256 devices in a mesh: dp: 2 (over x_lo), tile: 128 (over z, y, x_hi, core).
Axes of the slice: x: 4 (x_hi: 2, x_lo: 2; x = x_hi * 2 + x_lo), y: 4, z: 8, core: 2. Of those that a mesh axis runs over, the one named last changes fastest.
Arguments:
- features: bfloat16 [8, 2, 16384, 1024], P('dp', None, 'tile'), may hold values from -6 to 6
- proj_weight: bfloat16 [2, 1024, 256], replicated, may hold values from -0.1875 to 0.1875
- conv_weight: bfloat16 [2, 3, 3, 256, 256], replicated, may hold values from -0.125 to 0.125
- saved: bfloat16 [8, 2, 1024, 16, 256], P('dp', None, 'tile'), may hold values from -6 to 6
- cotangent: bfloat16 [8, 2048, 32, 256], P('dp', 'tile'), may hold values from -6 to 6
Outputs:
- feature_grad: bfloat16 [8, 2, 16384, 1024], P('dp', None, 'tile')
- head_grad: float32 [6656, 256], P(('dp', 'tile'))
The draws below stay inside these ranges and needn't reach their ends.
All inputs are finite; a program needn't handle non-finite values.
Results may differ from the reference program's by a relative error of at most 0.0057.
Values may be sent and summed in bfloat16 or wider, within the bound.
A program may use at most 128 MiB of HBM per device.

```python
import math
import jax
import jax.numpy as jnp
from jax import lax

D = 1024
C = 256
DEPTHS = 2
TILE_H = 8
TILE_W = 16
TILE_COLS = 8
IMAGES = 8
GRID_H = 128
GRID_W = 128
TOKENS = 16384
N_TILE = 128


def levels(own_key, shape, split, least, high):
    level, own = 1.0, jax.random.fold_in(own_key, 6)
    for axis_at, shards_of in split:
        draws = jnp.exp(jax.random.uniform(jax.random.fold_in(own, axis_at), (shards_of,), jnp.float32, least / len(split), high / len(split)))
        level = level * jnp.repeat(draws, shape[axis_at] // shards_of).reshape([-1 if axis == axis_at else 1 for axis in range(len(shape))])
    return level


def normal_values(key, extent, scale, bound, cuts=(), dtype=jnp.bfloat16):
    loudness = levels(key, extent, cuts, -0.22, 0.18) if cuts else 1.0
    array = jax.random.normal(key, extent, jnp.float32) * scale * loudness
    return jnp.minimum(jnp.maximum(array, -bound), bound).astype(dtype)


def setup_inputs(seed: int = 0) -> dict:
    arg_keys = jax.random.split(jax.random.key(seed), 6)
    features = normal_values(arg_keys[0], (IMAGES, DEPTHS, TOKENS, D), 1.0, 6.0, ((0, 2), (2, 128)))
    proj_weight = normal_values(arg_keys[1], (DEPTHS, D, C), D ** -0.5, 0.1875)
    conv_weight = normal_values(arg_keys[2], (DEPTHS, 3, 3, C, C), (9 * C) ** -0.5, 0.125)
    saved = normal_values(arg_keys[3], (IMAGES, DEPTHS, N_TILE * TILE_H, TILE_W, C), 1.0, 6.0, ((0, 2), (2, 128)))
    cotangent = normal_values(arg_keys[4], (IMAGES, N_TILE * 2 * TILE_H, 2 * TILE_W, C), 1.0, 6.0, ((0, 2), (1, 128)))
    return dict(features=features, proj_weight=proj_weight, conv_weight=conv_weight, saved=saved, cotangent=cotangent)


def untile(field_in, cell_rows, cell_cols):
    leading = field_in.shape[0]
    channels = field_in.shape[-1]
    blocks = field_in.reshape(leading, N_TILE // TILE_COLS, TILE_COLS, cell_rows, cell_cols, channels)
    order = [column ^ column >> 1 for column in range(TILE_COLS)]
    blocks = blocks[:, :, order]
    blocks = blocks.transpose(0, 1, 3, 2, 4, 5)
    return blocks.reshape(leading, N_TILE // TILE_COLS * cell_rows, TILE_COLS * cell_cols, channels)

def pool(values_in, along_dim, lo_edge, hi_edge):
    cell_count = (values_in.shape[along_dim] - 2) // 2
    even_part = lax.slice_in_dim(values_in, 1, 2 * cell_count + 1, 2, along_dim)
    odd_part = lax.slice_in_dim(values_in, 2, 2 * cell_count + 2, 2, along_dim)
    before = lax.slice_in_dim(values_in, 0, 2 * cell_count, 2, along_dim)
    after = lax.slice_in_dim(values_in, 3, 2 * cell_count + 2, 2, along_dim)
    target_shape = [1] * values_in.ndim
    target_shape[along_dim] = cell_count
    iota_pos = lax.broadcasted_iota(jnp.int32, tuple(target_shape), along_dim)
    at_first = jnp.logical_and(iota_pos == 0, lo_edge)
    at_last = jnp.logical_and(iota_pos == cell_count - 1, hi_edge)
    result = 0.75 * (even_part + odd_part) + 0.25 * (before + after)
    result = result + 0.25 * jnp.where(at_first, even_part, jnp.zeros_like(even_part))
    result = result + 0.25 * jnp.where(at_last, odd_part, jnp.zeros_like(odd_part))
    return result

def reference(features, proj_weight, conv_weight, saved, cotangent):
    grid_grad = untile(cotangent.astype(jnp.float32), 2 * TILE_H, 2 * TILE_W)
    padded = jnp.pad(grid_grad, ((0, 0), (1, 1), (1, 1), (0, 0)))
    row_pooled = pool(padded, 1, True, True)
    pooled = pool(row_pooled, 2, True, True).astype(jnp.bfloat16)
    dpad = jnp.pad(pooled, ((0, 0), (1, 1), (1, 1), (0, 0)))
    activ = untile(saved.reshape(IMAGES * DEPTHS, N_TILE * TILE_H, TILE_W, C), TILE_H, TILE_W)
    activ = activ.reshape(IMAGES, DEPTHS, GRID_H, GRID_W, C)
    grads_out = []
    proj_rows = []
    conv_rows = []
    for depth_index in range(DEPTHS):
        summed = jnp.zeros((IMAGES * GRID_H * GRID_W, C), jnp.float32)
        flat_act = activ[:, depth_index].reshape(-1, C)
        for kernel_row in range(3):
            for kernel_col in range(3):
                shifted = dpad[:, 2 - kernel_row:2 - kernel_row + GRID_H, 2 - kernel_col:2 - kernel_col + GRID_W]
                shifted = shifted.reshape(-1, C)
                summed = summed + jnp.dot(shifted, conv_weight[depth_index, kernel_row, kernel_col].T, preferred_element_type=jnp.float32)
                conv_rows.append(jnp.dot(flat_act.T, shifted, preferred_element_type=jnp.float32))
        token_grad = summed.astype(jnp.bfloat16)
        feat_grad = jnp.dot(token_grad, proj_weight[depth_index].T, preferred_element_type=jnp.float32)
        grads_out.append(feat_grad.astype(jnp.bfloat16).reshape(IMAGES, TOKENS, D))
        proj_rows.append(jnp.dot(features[:, depth_index].reshape(-1, D).T, token_grad, preferred_element_type=jnp.float32))
    feature_grad = jnp.stack(grads_out, axis=1)
    head_grad = jnp.concatenate(proj_rows + conv_rows, axis=0) * (1.0 / math.sqrt(IMAGES * TOKENS))
    return (feature_grad, head_grad)
```

```python
import math

import jax
import jax.numpy as jnp
import ml_dtypes
import numpy as np
from jax import lax
from jax.experimental import pallas as pl
from jax.experimental.pallas import tpu as pltpu
from jax.sharding import PartitionSpec as P

MESH = pl.DeviceIdType.MESH
BF = jnp.bfloat16
F32 = jnp.float32

DIRS = ((-1, 0), (1, 0), (0, -1), (0, 1), (-1, -1), (-1, 1), (1, -1), (1, 1))
MAIN = (32, 32, 16, 16, 0, 0, 0, 0)
SIZE = tuple(4 * m + 16 for m in MAIN)
START = tuple(sum(SIZE[:d]) for d in range(8))
MAIN_AT = (0, 32, 64, 80)

CHUNK = 416
HEAD_ROWS = 26


def weight(cell, fine, cells, first, last):
    at = fine - 2 * cell
    value = 0.75 if at in (0, 1) else 0.25 if at in (-1, 2) else 0.0
    if first and cell == 0 and fine == 0:
        value += 0.25
    if last and cell == cells - 1 and fine == 2 * cells - 1:
        value += 0.25
    return value


def halo_cells(d):
    dr, dc = DIRS[d]
    rows = {1: [-1, 0], -1: [8, 7], 0: list(range(8))}[dr]
    cols = {1: [-1, 0], -1: [16, 15], 0: list(range(16))}[dc]
    if dr and dc:
        return [], [(j, w) for j in rows for w in cols]
    main = [(j, w) for j in rows for w in cols]
    if dr:
        corner = [(j, w) for j in rows for w in (-1, 16)]
    else:
        corner = [(j, w) for j in (-1, 8) for w in cols]
    return main, corner


def tables():
    send = np.zeros((9, 128, 512), np.float32)
    take = np.zeros((9, 480, 640), np.float32)
    for place in range(9):
        top, bottom = place // 3 == 0, place // 3 == 2
        left, right = place % 3 == 0, place % 3 == 2
        row_w = np.array([[weight(j, r, 8, top, bottom) for r in range(16)] for j in range(-1, 9)])
        col_w = np.array([[weight(w, c, 16, left, right) for c in range(32)] for w in range(-1, 17)])

        def line(j, w):
            return np.outer(row_w[j + 1], col_w[w + 1]).reshape(512)

        for d, (dr, dc) in enumerate(DIRS):
            main, corner = halo_cells(d)
            for m, (j, w) in enumerate(main):
                send[place, MAIN_AT[d] + m] = line(j + 8 * dr, w + 16 * dc)
            for m, (j, w) in enumerate(corner):
                send[place, 96 + 4 * d + m] = line(j + 8 * dr, w + 16 * dc)

        def outside(j, w):
            return (j < 0 and top) or (j > 7 and bottom) or (w < 0 and left) or (w > 15 and right)

        for shift in range(3):
            for jr in range(10):
                for ww in range(16):
                    j, w = jr - 1, shift + ww - 1
                    if not outside(j, w):
                        take[place, shift * 160 + jr * 16 + ww, :512] = line(j, w)
            for d in range(8):
                main, corner = halo_cells(d)
                at = [(512 + MAIN_AT[d] + m, cell) for m, cell in enumerate(main)] if main else []
                at += [(608 + 4 * d + m, cell) for m, cell in enumerate(corner)]
                for column, (j, w) in at:
                    ww = w + 1 - shift
                    if 0 <= ww < 16 and not outside(j, w):
                        take[place, shift * 160 + (j + 1) * 16 + ww, column] = 1.0
    order = np.zeros((128, 128), np.float32)
    for i in range(4):
        for d in range(8):
            for cell in range(4):
                order[d * 16 + i * 4 + cell, i * 32 + d * 4 + cell] = 1.0
    as_bf16 = [a.astype(ml_dtypes.bfloat16) for a in (send, take, np.stack([order, order.T]))]
    return as_bf16


def mm(a, b):
    return jnp.dot(a, b, preferred_element_type=F32)


def mm_t(a, b):
    return lax.dot_general(a, b, (((1,), (1,)), ((), ())), preferred_element_type=F32)


def kernel(
    cot_hbm, saved_hbm, feat_hbm, w_hbm, send_hbm, take_hbm, order_hbm,
    tok_out, head_out,
    cot, saved, feat, wconv, send_m, take_m, order_m,
    saved_t, feat_t, halo_out, halo_in, corner, acc, pooled, grad_acc, grad, tok,
    head, send_c, recv_c, part, send_1, recv_1, send_2, recv_2, last, send_3, recv_3,
    load_sem, halo_ss, halo_rs, tok_ss, tok_rs, c_ss, c_rs, ss_1, rs_1, ss_2, rs_2, ss_3, rs_3, out_sem,
):
    dp = lax.axis_index("dp")
    tile = lax.axis_index("tile")
    z, y, xh, core = tile // 16, (tile // 4) % 4, (tile // 2) % 2, tile % 2
    x = xh * 2 + dp
    g, row = tile % 8, tile // 8
    g0, g1, g2 = g % 2, (g // 2) % 2, g // 4
    col = g2 * 4 + (g2 + g1) % 2 * 2 + (g2 + g1 + g0) % 2
    a = jnp.where(core == 0, x, y)
    b = jnp.where(core == 0, y, x)

    def gray(c):
        c0, c1, c2 = c % 2, (c // 2) % 2, c // 4
        return c2 * 4 + (c2 + c1) % 2 * 2 + (c1 + c0) % 2

    def in_plane(to_a, to_b):
        to_x = jnp.where(core == 0, to_a, to_b)
        to_y = jnp.where(core == 0, to_b, to_a)
        return {"dp": to_x % 2, "tile": z * 16 + to_y * 4 + to_x // 2 * 2 + core}

    def remote(src, dst, send_sem, recv_sem, device):
        return pltpu.make_async_remote_copy(
            src_ref=src, dst_ref=dst, send_sem=send_sem, recv_sem=recv_sem,
            device_id=device, device_id_type=MESH,
        )

    place = (
        jnp.where(row == 0, 0, jnp.where(row == 15, 2, 1)) * 3
        + jnp.where(col == 0, 0, jnp.where(col == 7, 2, 1))
    )
    loads = [
        pltpu.make_async_copy(src, dst, load_sem.at[n])
        for n, (src, dst) in enumerate([
            (cot_hbm, cot), (send_hbm.at[place], send_m), (order_hbm, order_m),
            (take_hbm.at[place], take_m), (saved_hbm, saved), (w_hbm, wconv), (feat_hbm, feat),
        ])
    ]
    for load in loads:
        load.start()

    for n in range(3):
        loads[n].wait()
    for i in range(4):
        r = mm(send_m[...], cot[i]).astype(BF)
        for d in range(4):
            m = MAIN[d]
            halo_out[START[d] + i * m : START[d] + (i + 1) * m, :] = r[MAIN_AT[d] : MAIN_AT[d] + m]
        corner[i * 32 : (i + 1) * 32, :] = r[96:128]
    corners = mm(order_m[0], corner[...]).astype(BF)
    for d in range(8):
        halo_out[START[d] + 4 * MAIN[d] : START[d] + SIZE[d], :] = corners[d * 16 : d * 16 + 16]

    def halo(d):
        dr, dc = DIRS[d]
        there = jnp.clip(row + dr, 0, 15) * 8 + gray(jnp.clip(col + dc, 0, 7))
        return remote(
            halo_out.at[START[d] : START[d] + SIZE[d]], halo_in.at[START[d] : START[d] + SIZE[d]],
            halo_ss.at[d], halo_rs.at[d], {"tile": there},
        )

    def has(dr, dc):
        to_row, to_col = row + dr, col + dc
        ok = jnp.logical_and(to_row >= 0, to_row < 16)
        return jnp.logical_and(ok, jnp.logical_and(to_col >= 0, to_col < 8))

    for d in range(8):
        dr, dc = DIRS[d]

        @pl.when(has(dr, dc))
        def _():
            halo(d).start()

        @pl.when(jnp.logical_not(has(-dr, -dc)))
        def _():
            halo_in[START[d] : START[d] + SIZE[d], :] = jnp.zeros((SIZE[d], 256), BF)

    loads[3].wait()
    for i in range(4):
        acc[i] = mm(take_m[:, :512], cot[i])
    loads[4].wait()
    for k in range(2):
        for i in range(4):
            saved_t[k * 256 : (k + 1) * 256, i * 128 : (i + 1) * 128] = saved[i, k].T

    for d in range(8):
        dr, dc = DIRS[d]

        @pl.when(has(-dr, -dc))
        def _():
            halo(d).wait_recv()

    for d in range(8):
        at = START[d] + 4 * MAIN[d]
        corner[d * 16 : d * 16 + 16, :] = halo_in[at : at + 16, :]
    corners = mm(order_m[1], corner[...]).astype(BF)
    for i in range(4):
        parts = [halo_in[START[d] + i * MAIN[d] : START[d] + (i + 1) * MAIN[d], :] for d in range(4)]
        ring = jnp.concatenate(parts + [corners[i * 32 : (i + 1) * 32]], axis=0)
        full = (acc[i] + mm(take_m[:, 512:], ring)).astype(BF)
        for shift in range(3):
            pooled[shift, i] = full[shift * 160 : (shift + 1) * 160]

    def tap(t):
        u, v = t // 3, t % 3
        return pooled[2 - v, :, (2 - u) * 16 : (2 - u) * 16 + 128, :].reshape(512, 256)

    loads[5].wait()
    for k in range(2):
        for t in range(9):
            term = mm_t(tap(t), wconv[k * 9 + t])
            if t == 0:
                grad_acc[...] = term
            elif t < 8:
                grad_acc[...] += term
            else:
                grad[k] = (grad_acc[...] + term).astype(BF).reshape(4, 128, 256)

    def regroup(n):
        there = (g + n) % 8
        return remote(
            grad.at[:, :, pl.ds(pl.multiple_of(there * 16, 16), 16)],
            tok.at[:, :, pl.ds(pl.multiple_of(col * 16, 16), 16)],
            tok_ss.at[n], tok_rs.at[n], {"tile": row * 8 + there},
        )

    for n in range(1, 8):
        regroup(n).start()
    tok[:, :, pl.ds(pl.multiple_of(col * 16, 16), 16)] = grad[:, :, pl.ds(pl.multiple_of(g * 16, 16), 16)]

    mine = pl.ds(pl.multiple_of(core * 128, 128), 128)
    theirs = pl.ds(pl.multiple_of((1 - core) * 128, 128), 128)
    pair = {"tile": tile + 1 - 2 * core}

    def swap(q):
        return remote(send_c.at[q], recv_c.at[q], c_ss.at[q], c_rs.at[q], pair)

    def first(q, to_a):
        slot = (to_a - a + 4) % 4
        return remote(
            send_1.at[q], recv_1.at[q // 4, slot - 1], ss_1.at[q], rs_1.at[q // 4, slot - 1], in_plane(to_a, b)
        )

    def ready(q):
        send_c[q] = head[q * CHUNK : (q + 1) * CHUNK, theirs].astype(BF)
        swap(q).start()

    def reduced(q):
        swap(q).wait_recv()
        total = head[q * CHUNK : (q + 1) * CHUNK, mine] + recv_c[q].astype(F32)
        part[q] = total
        send_1[q] = total.astype(BF)

        @pl.when(a != q % 4)
        def _():
            first(q, q % 4).start()

    for k in range(2):
        for t in range(9):
            at = 2048 + (k * 9 + t) * 256
            head[at : at + 256, :] = mm(saved_t[k * 256 : (k + 1) * 256, :], tap(t))
        for q in (range(5, 10), range(10, 16))[k]:
            ready(q)
    loads[6].wait()
    for k in range(2):
        for i in range(4):
            feat_t[k * 1024 : (k + 1) * 1024, i * 128 : (i + 1) * 128] = feat[i, k].T
    for q in range(5, 16):
        reduced(q)

    for n in range(1, 8):
        regroup(n).wait_recv()
    out_copy = pltpu.make_async_copy(tok, tok_out, out_sem)
    out_copy.start()
    for k in range(2):
        for h in range(4):
            at = k * 1024 + h * 256
            head[at : at + 256, :] = mm(feat_t[at : at + 256, :], tok[k].reshape(512, 256))
        for q in (range(0, 2), range(2, 5))[k]:
            ready(q)
    for q in range(0, 5):
        reduced(q)

    def second(to_b):
        slot = (to_b - b + 4) % 4
        return remote(
            send_2.at[to_b], recv_2.at[slot - 1], ss_2.at[slot - 1], rs_2.at[slot - 1], in_plane(a, to_b)
        )

    for j in (3, 2, 1, 0):
        total = part[j * 4 + a]
        for s in range(3):
            first(j * 4 + 0, (a + s + 1) % 4).wait_recv()
            total = total + recv_1[j, s].astype(F32)
        part[j * 4 + a] = total
        send_2[j] = total.astype(BF)

        @pl.when(b != j)
        def _():
            second(j).start()

    total = part[b * 4 + a]
    for s in range(3):
        second((b + s + 1) % 4).wait_recv()
        total = total + recv_2[s].astype(F32)
    last[0:CHUNK, :] = total
    last[CHUNK:432, :] = jnp.zeros((16, 128), F32)
    for p in range(16):
        send_3[p] = last[p * HEAD_ROWS : p * HEAD_ROWS + 32, :].astype(BF)

    held = b * 4 + a
    own = dp * 8 + z

    def third(p):
        return remote(
            send_3.at[p], recv_3.at[z, core], ss_3.at[p], rs_3.at[z, core],
            {"dp": held // 8, "tile": held % 8 * 16 + p},
        )

    def to_self(p):
        return jnp.logical_and(held == own, tile % 16 == p)

    for p in range(16):

        @pl.when(jnp.logical_not(to_self(p)))
        def _():
            third(p).start()

        @pl.when(to_self(p))
        def _():
            recv_3[z, core] = send_3[p]

    total = [None, None]
    for cc in range(2):
        from_x = own % 4 if cc == 0 else own // 4
        from_y = own // 4 if cc == 0 else own % 4
        for zz in range(8):
            source = zz * 16 + from_y * 4 + from_x // 2 * 2 + cc
            itself = jnp.logical_and(from_x % 2 == dp, source == tile)

            @pl.when(jnp.logical_not(itself))
            def _():
                remote(
                    send_3.at[0], recv_3.at[zz, cc], ss_3.at[0], rs_3.at[zz, cc],
                    {"dp": from_x % 2, "tile": source},
                ).wait_recv()

            piece = recv_3[zz, cc].astype(F32)
            total[cc] = piece if zz == 0 else total[cc] + piece
    scale = 1.0 / math.sqrt(8 * 16384)
    for cc in range(2):
        head_out[:, cc * 128 : (cc + 1) * 128] = total[cc][:HEAD_ROWS] * scale

    for d in range(8):

        @pl.when(has(*DIRS[d]))
        def _():
            halo(d).wait_send()

    for n in range(1, 8):
        regroup(n).wait_send()
    for q in range(16):
        swap(q).wait_send()

        @pl.when(a != q % 4)
        def _():
            first(q, q % 4).wait_send()

    for s in range(3):
        second((b + s + 1) % 4).wait_send()
    for p in range(16):

        @pl.when(jnp.logical_not(to_self(p)))
        def _():
            third(p).wait_send()

    out_copy.wait()


def per_device(features, proj_weight, conv_weight, saved, cotangent):
    send, take, order = (jnp.asarray(t) for t in tables())
    hbm = pl.BlockSpec(memory_space=pl.ANY)
    dma = pltpu.SemaphoreType.DMA
    vmem = pltpu.VMEM
    tok, head = pl.pallas_call(
        kernel,
        out_shape=(
            jax.ShapeDtypeStruct((2, 4, 128, 256), BF),
            jax.ShapeDtypeStruct((HEAD_ROWS, 256), F32),
        ),
        in_specs=[hbm] * 7,
        out_specs=(hbm, pl.BlockSpec(memory_space=pltpu.VMEM)),
        scratch_shapes=[
            vmem((4, 512, 256), BF), vmem((4, 2, 128, 256), BF), vmem((4, 2, 128, 1024), BF),
            vmem((18, 256, 256), BF), vmem((128, 512), BF), vmem((480, 640), BF), vmem((2, 128, 128), BF),
            vmem((512, 512), BF), vmem((2048, 512), BF), vmem((512, 256), BF), vmem((512, 256), BF),
            vmem((128, 256), BF), vmem((4, 480, 256), F32), vmem((3, 4, 160, 256), BF),
            vmem((512, 256), F32), vmem((2, 4, 128, 256), BF), vmem((2, 4, 128, 256), BF),
            vmem((6656, 256), F32), vmem((16, CHUNK, 128), BF), vmem((16, CHUNK, 128), BF),
            vmem((16, CHUNK, 128), F32), vmem((16, CHUNK, 128), BF), vmem((4, 3, CHUNK, 128), BF),
            vmem((4, CHUNK, 128), BF), vmem((3, CHUNK, 128), BF), vmem((432, 128), F32),
            vmem((16, 32, 128), BF), vmem((8, 2, 32, 128), BF),
            dma((7,)), dma((8,)), dma((8,)), dma((8,)), dma((8,)), dma((16,)), dma((16,)),
            dma((16,)), dma((4, 3)), dma((3,)), dma((3,)), dma((16,)), dma((8, 2)), dma,
        ],
        compiler_params=pltpu.CompilerParams(has_side_effects=True, vmem_limit_bytes=56 * 2**20),
        cost_estimate=pl.CostEstimate(flops=3_000_000_000, bytes_accessed=9_000_000, transcendentals=0),
        name="head_backward",
    )(
        cotangent.reshape(4, 512, 256),
        saved.reshape(4, 2, 128, 256),
        features,
        conv_weight.reshape(18, 256, 256),
        send,
        take,
        order,
    )
    feature_grad = jnp.einsum("kinc,kdc->iknd", tok, proj_weight, preferred_element_type=F32)
    return feature_grad.astype(BF), head


def solution(mesh):
    in_specs = (
        P("dp", None, "tile", None),
        P(),
        P(),
        P("dp", None, "tile", None, None),
        P("dp", "tile", None, None),
    )
    out_specs = (P("dp", None, "tile", None), P(("dp", "tile"), None))
    return jax.shard_map(
        per_device, mesh=mesh, in_specs=in_specs, out_specs=out_specs, check_vma=False
    )
```

```python
import math

import jax
import jax.numpy as jnp
import ml_dtypes
import numpy as np
from jax import lax
from jax.experimental import pallas as pl
from jax.experimental.pallas import tpu as pltpu
from jax.sharding import PartitionSpec as P

MESH = pl.DeviceIdType.MESH
BF = jnp.bfloat16
F32 = jnp.float32

DIRS = ((-1, 0), (1, 0), (0, -1), (0, 1), (-1, -1), (-1, 1), (1, -1), (1, 1))
MAIN = (32, 32, 16, 16, 0, 0, 0, 0)
SIZE = tuple(4 * m + 16 for m in MAIN)
START = tuple(sum(SIZE[:d]) for d in range(8))
MAIN_AT = (0, 32, 64, 80)

CHUNK = 416
HEAD_ROWS = 26


def weight(cell, fine, cells, first, last):
    at = fine - 2 * cell
    value = 0.75 if at in (0, 1) else 0.25 if at in (-1, 2) else 0.0
    if first and cell == 0 and fine == 0:
        value += 0.25
    if last and cell == cells - 1 and fine == 2 * cells - 1:
        value += 0.25
    return value


def halo_cells(d):
    dr, dc = DIRS[d]
    rows = {1: [-1, 0], -1: [8, 7], 0: list(range(8))}[dr]
    cols = {1: [-1, 0], -1: [16, 15], 0: list(range(16))}[dc]
    if dr and dc:
        return [], [(j, w) for j in rows for w in cols]
    main = [(j, w) for j in rows for w in cols]
    if dr:
        corner = [(j, w) for j in rows for w in (-1, 16)]
    else:
        corner = [(j, w) for j in (-1, 8) for w in cols]
    return main, corner


def tables():
    send = np.zeros((9, 128, 512), np.float32)
    take = np.zeros((9, 480, 640), np.float32)
    for place in range(9):
        top, bottom = place // 3 == 0, place // 3 == 2
        left, right = place % 3 == 0, place % 3 == 2
        row_w = np.array([[weight(j, r, 8, top, bottom) for r in range(16)] for j in range(-1, 9)])
        col_w = np.array([[weight(w, c, 16, left, right) for c in range(32)] for w in range(-1, 17)])

        def line(j, w):
            return np.outer(row_w[j + 1], col_w[w + 1]).reshape(512)

        for d, (dr, dc) in enumerate(DIRS):
            main, corner = halo_cells(d)
            for m, (j, w) in enumerate(main):
                send[place, MAIN_AT[d] + m] = line(j + 8 * dr, w + 16 * dc)
            for m, (j, w) in enumerate(corner):
                send[place, 96 + 4 * d + m] = line(j + 8 * dr, w + 16 * dc)

        def outside(j, w):
            return (j < 0 and top) or (j > 7 and bottom) or (w < 0 and left) or (w > 15 and right)

        for shift in range(3):
            for jr in range(10):
                for ww in range(16):
                    j, w = jr - 1, shift + ww - 1
                    if not outside(j, w):
                        take[place, shift * 160 + jr * 16 + ww, :512] = line(j, w)
            for d in range(8):
                main, corner = halo_cells(d)
                at = [(512 + MAIN_AT[d] + m, cell) for m, cell in enumerate(main)] if main else []
                at += [(608 + 4 * d + m, cell) for m, cell in enumerate(corner)]
                for column, (j, w) in at:
                    ww = w + 1 - shift
                    if 0 <= ww < 16 and not outside(j, w):
                        take[place, shift * 160 + (j + 1) * 16 + ww, column] = 1.0
    order = np.zeros((128, 128), np.float32)
    for i in range(4):
        for d in range(8):
            for cell in range(4):
                order[d * 16 + i * 4 + cell, i * 32 + d * 4 + cell] = 1.0
    as_bf16 = [a.astype(ml_dtypes.bfloat16) for a in (send, take, np.stack([order, order.T]))]
    return as_bf16


def mm(a, b):
    return jnp.dot(a, b, preferred_element_type=F32)


def mm_t(a, b):
    return lax.dot_general(a, b, (((1,), (1,)), ((), ())), preferred_element_type=F32)


def kernel(
    cot_hbm, saved_hbm, feat_hbm, w_hbm, proj_hbm, send_hbm, take_hbm, order_hbm,
    fg_out, head_out,
    cot, saved, feat, wconv, proj, send_m, take_m, order_m,
    saved_t, feat_t, halo_out, halo_in, corner, acc, pooled, grad_acc, grad, tok, fg,
    head, send_c, recv_c, part, split_1, send_1, recv_1, kept_1, split_2, send_2, recv_2, last, send_3, recv_3,
    load_sem, halo_ss, halo_rs, tok_ss, tok_rs, c_ss, c_rs, ss_1, rs_1, ss_2, rs_2, ss_3, rs_3, out_sem,
):
    dp = lax.axis_index("dp")
    tile = lax.axis_index("tile")
    z, y, xh, core = tile // 16, (tile // 4) % 4, (tile // 2) % 2, tile % 2
    x = xh * 2 + dp
    g, row = tile % 8, tile // 8
    g0, g1, g2 = g % 2, (g // 2) % 2, g // 4
    col = g2 * 4 + (g2 + g1) % 2 * 2 + (g2 + g1 + g0) % 2
    a = jnp.where(core == 0, x, y)
    b = jnp.where(core == 0, y, x)

    def gray(c):
        c0, c1, c2 = c % 2, (c // 2) % 2, c // 4
        return c2 * 4 + (c2 + c1) % 2 * 2 + (c1 + c0) % 2

    def in_plane(to_a, to_b):
        to_x = jnp.where(core == 0, to_a, to_b)
        to_y = jnp.where(core == 0, to_b, to_a)
        return {"dp": to_x % 2, "tile": z * 16 + to_y * 4 + to_x // 2 * 2 + core}

    def remote(src, dst, send_sem, recv_sem, device):
        return pltpu.make_async_remote_copy(
            src_ref=src, dst_ref=dst, send_sem=send_sem, recv_sem=recv_sem,
            device_id=device, device_id_type=MESH,
        )

    place = (
        jnp.where(row == 0, 0, jnp.where(row == 15, 2, 1)) * 3
        + jnp.where(col == 0, 0, jnp.where(col == 7, 2, 1))
    )
    loads = [
        pltpu.make_async_copy(src, dst, load_sem.at[n])
        for n, (src, dst) in enumerate([
            (cot_hbm, cot), (send_hbm.at[place], send_m), (order_hbm, order_m),
            (take_hbm.at[place], take_m), (saved_hbm, saved), (w_hbm, wconv), (feat_hbm, feat),
            (proj_hbm, proj),
        ])
    ]
    for load in loads:
        load.start()

    barrier = pltpu.get_barrier_semaphore()

    def greet(device):
        pl.semaphore_signal(barrier, inc=1, device_id=device, device_id_type=MESH)

    def has(dr, dc):
        to_row, to_col = row + dr, col + dc
        ok = jnp.logical_and(to_row >= 0, to_row < 16)
        return jnp.logical_and(ok, jnp.logical_and(to_col >= 0, to_col < 8))

    def beside(dr, dc):
        return jnp.clip(row + dr, 0, 15) * 8 + gray(jnp.clip(col + dc, 0, 7))

    greeted = jnp.int32(0)
    for dr, dc in DIRS:
        if dr:

            @pl.when(has(dr, dc))
            def _():
                greet({"tile": beside(dr, dc)})

            greeted = greeted + has(dr, dc).astype(jnp.int32)
    for n in range(1, 8):
        greet({"tile": row * 8 + (g + n) % 8})
    for n in range(2):
        greet({"dp": 1 - dp, "tile": z * 16 + y * 4 + n * 2 + core})
        greet({"tile": z * 16 + (y // 2 * 2 + 2 + n) % 4 * 4 + xh * 2 + core})
    for n in range(1, 8):
        for c in range(2):
            greet({"tile": (z + n) % 8 * 16 + y * 4 + xh * 2 + c})
    greeted = greeted + 25

    for n in range(3):
        loads[n].wait()
    for i in range(4):
        r = mm(send_m[...], cot[i]).astype(BF)
        for d in range(4):
            m = MAIN[d]
            halo_out[START[d] + i * m : START[d] + (i + 1) * m, :] = r[MAIN_AT[d] : MAIN_AT[d] + m]
        corner[i * 32 : (i + 1) * 32, :] = r[96:128]
    corners = mm(order_m[0], corner[...]).astype(BF)
    for d in range(8):
        halo_out[START[d] + 4 * MAIN[d] : START[d] + SIZE[d], :] = corners[d * 16 : d * 16 + 16]

    def halo(d):
        return remote(
            halo_out.at[START[d] : START[d] + SIZE[d]], halo_in.at[START[d] : START[d] + SIZE[d]],
            halo_ss.at[d], halo_rs.at[d], {"tile": beside(*DIRS[d])},
        )

    pl.semaphore_wait(barrier, greeted)
    for d in range(8):
        dr, dc = DIRS[d]

        @pl.when(has(dr, dc))
        def _():
            halo(d).start()

        @pl.when(jnp.logical_not(has(-dr, -dc)))
        def _():
            halo_in[START[d] : START[d] + SIZE[d], :] = jnp.zeros((SIZE[d], 256), BF)

    loads[3].wait()
    for i in range(4):
        acc[i] = mm(take_m[:, :512], cot[i])
    loads[4].wait()
    for k in range(2):
        for i in range(4):
            saved_t[k * 256 : (k + 1) * 256, i * 128 : (i + 1) * 128] = saved[i, k].T

    for d in range(8):
        dr, dc = DIRS[d]

        @pl.when(has(-dr, -dc))
        def _():
            halo(d).wait_recv()

    for d in range(8):
        at = START[d] + 4 * MAIN[d]
        corner[d * 16 : d * 16 + 16, :] = halo_in[at : at + 16, :]
    corners = mm(order_m[1], corner[...]).astype(BF)
    for i in range(4):
        parts = [halo_in[START[d] + i * MAIN[d] : START[d] + (i + 1) * MAIN[d], :] for d in range(4)]
        ring = jnp.concatenate(parts + [corners[i * 32 : (i + 1) * 32]], axis=0)
        full = (acc[i] + mm(take_m[:, 512:], ring)).astype(BF)
        for shift in range(3):
            pooled[shift, i] = full[shift * 160 : (shift + 1) * 160]

    def tap(t):
        u, v = t // 3, t % 3
        return pooled[2 - v, :, (2 - u) * 16 : (2 - u) * 16 + 128, :].reshape(512, 256)

    loads[5].wait()
    for k in range(2):
        for t in range(9):
            term = mm_t(tap(t), wconv[k * 9 + t])
            if t == 0:
                grad_acc[...] = term
            elif t < 8:
                grad_acc[...] += term
            else:
                grad[k] = (grad_acc[...] + term).astype(BF).reshape(4, 128, 256)

    def regroup(n):
        there = (g + n) % 8
        return remote(
            grad.at[:, :, pl.ds(pl.multiple_of(there * 16, 16), 16)],
            tok.at[:, :, pl.ds(pl.multiple_of(col * 16, 16), 16)],
            tok_ss.at[n], tok_rs.at[n], {"tile": row * 8 + there},
        )

    for n in range(1, 8):
        regroup(n).start()
    tok[:, :, pl.ds(pl.multiple_of(col * 16, 16), 16)] = grad[:, :, pl.ds(pl.multiple_of(g * 16, 16), 16)]

    mine = pl.ds(pl.multiple_of(core * 128, 128), 128)
    theirs = pl.ds(pl.multiple_of((1 - core) * 128, 128), 128)
    pair_device = {"tile": tile + 1 - 2 * core}

    def swap(q):
        return remote(send_c.at[q], recv_c.at[q], c_ss.at[q], c_rs.at[q], pair_device)

    def to_first(pair, n):
        return jnp.where(core == 0, pair // 4 + n % 2 * 2, n)

    def first(pair, n):
        to_a = to_first(pair, n)
        slot = jnp.where(core == 0, pair % 4 * 2 + n // 2, pair)
        step = (to_a - a + 3) % 4
        return remote(
            send_1.at[pair, n], recv_1.at[slot, step], ss_1.at[pair, n], rs_1.at[slot, step], in_plane(to_a, b)
        )

    def ready(q):
        send_c[q] = head[q * CHUNK : (q + 1) * CHUNK, theirs].astype(BF)
        swap(q).start()

    def reduced(pair):
        for q in (2 * pair, 2 * pair + 1):
            swap(q).wait_recv()
            part[q] = head[q * CHUNK : (q + 1) * CHUNK, mine] + recv_c[q].astype(F32)

        @pl.when(core == 0)
        def _():
            for n in range(4):
                for p in range(4):
                    at = p * 104 + n % 2 * 52
                    split_1[pair, n, p * 52 : p * 52 + 52, :] = part[2 * pair + n // 2, at : at + 52, :]

        @pl.when(core == 1)
        def _():
            for n in range(4):
                for h in range(2):
                    split_1[pair, n, h * 104 : h * 104 + 104, :] = part[2 * pair + h, n * 104 : n * 104 + 104, :]

        for n in range(4):
            send_1[pair, n] = split_1[pair, n].astype(BF)

            @pl.when(a != to_first(pair, n))
            def _():
                first(pair, n).start()

    for k in (1, 0):
        for t in range(9):
            at = 2048 + (k * 9 + t) * 256
            head[at : at + 256, :] = mm(saved_t[k * 256 : (k + 1) * 256, :], tap(t))
        for q in (range(5, 11), range(11, 16))[k]:
            ready(q)
    loads[6].wait()
    for k in range(2):
        for i in range(4):
            feat_t[k * 1024 : (k + 1) * 1024, i * 128 : (i + 1) * 128] = feat[i, k].T
    for pair in (6, 7, 5, 4, 3):
        reduced(pair)

    for n in range(1, 8):
        regroup(n).wait_recv()
    for k in range(2):
        for h in range(4):
            at = k * 1024 + h * 256
            head[at : at + 256, :] = mm(feat_t[at : at + 256, :], tok[k].reshape(512, 256))
        for q in (range(0, 2), range(2, 5))[k]:
            ready(q)
    for pair in (0, 1, 2):
        reduced(pair)

    loads[7].wait()
    for i in range(4):
        for k in range(2):
            fg[i, k] = mm_t(tok[k, i], proj[k]).astype(BF)
    out_copy = pltpu.make_async_copy(fg, fg_out, out_sem)
    out_copy.start()

    def second(to_b):
        step = (to_b - b + 3) % 4
        return remote(
            send_2.at[to_b], recv_2.at[step], ss_2.at[step], rs_2.at[step], in_plane(a, to_b)
        )

    for e in (7, 6, 5, 4, 3, 2, 1, 0):
        pair = jnp.where(core == 0, a % 2 * 4 + e // 2, e)
        n = jnp.where(core == 0, e % 2 * 2 + a // 2, a)
        total = split_1[pair, n]
        for s in range(3):
            remote(
                send_1.at[0, 0], recv_1.at[e, s], ss_1.at[0, 0], rs_1.at[e, s], pair_device
            ).wait_recv()
            total = total + recv_1[e, s].astype(F32)
        kept_1[e] = total

    @pl.when(core == 0)
    def _():
        for j in range(4):
            for e in range(8):
                split_2[j, e * 52 : e * 52 + 52, :] = kept_1[e, j * 52 : j * 52 + 52, :]

    @pl.when(core == 1)
    def _():
        for j in range(4):
            for p in range(8):
                at = p % 2 * 104 + j // 2 * 52
                split_2[j, p * 52 : p * 52 + 52, :] = kept_1[j % 2 * 4 + p // 2, at : at + 52, :]

    for j in range(4):
        send_2[j] = split_2[j].astype(BF)

        @pl.when(b != j)
        def _():
            second(j).start()

    total = split_2[b]
    for s in range(3):
        second((b + s + 1) % 4).wait_recv()
        total = total + recv_2[s].astype(F32)
    last[0:CHUNK, :] = total
    last[CHUNK:432, :] = jnp.zeros((16, 128), F32)

    def third(p):
        return remote(
            send_3.at[p], recv_3.at[z, core], ss_3.at[p], rs_3.at[z, core],
            {"tile": p // 2 * 16 + y * 4 + xh * 2 + p % 2},
        )

    def to_self(p):
        return jnp.logical_and(z == p // 2, core == p % 2)

    for p in range(16):
        send_3[p] = last[p * HEAD_ROWS : p * HEAD_ROWS + 32, :].astype(BF)

        @pl.when(jnp.logical_not(to_self(p)))
        def _():
            third(p).start()

        @pl.when(to_self(p))
        def _():
            recv_3[z, core] = send_3[p]

    scale = 1.0 / math.sqrt(8 * 16384)
    for c in range(2):
        total = jnp.zeros((32, 128), F32)
        for zz in range(8):

            @pl.when(jnp.logical_not(to_self(zz * 2 + c)))
            def _():
                remote(
                    send_3.at[0], recv_3.at[zz, c], ss_3.at[0], rs_3.at[zz, c], pair_device
                ).wait_recv()

            total = total + recv_3[zz, c].astype(F32)
        head_out[:, c * 128 : (c + 1) * 128] = total[:HEAD_ROWS] * scale

    for d in range(8):

        @pl.when(has(*DIRS[d]))
        def _():
            halo(d).wait_send()

    for n in range(1, 8):
        regroup(n).wait_send()
    for q in range(16):
        swap(q).wait_send()
    for pair in range(8):
        for n in range(4):

            @pl.when(a != to_first(pair, n))
            def _():
                first(pair, n).wait_send()

    for s in range(3):
        second((b + s + 1) % 4).wait_send()
    for p in range(16):

        @pl.when(jnp.logical_not(to_self(p)))
        def _():
            third(p).wait_send()

    out_copy.wait()


def per_device(features, proj_weight, conv_weight, saved, cotangent):
    send, take, order = (jnp.asarray(t) for t in tables())
    hbm = pl.BlockSpec(memory_space=pl.ANY)
    dma = pltpu.SemaphoreType.DMA
    vmem = pltpu.VMEM
    return pl.pallas_call(
        kernel,
        out_shape=(
            jax.ShapeDtypeStruct((4, 2, 128, 1024), BF),
            jax.ShapeDtypeStruct((HEAD_ROWS, 256), F32),
        ),
        in_specs=[hbm] * 8,
        out_specs=(hbm, pl.BlockSpec(memory_space=pltpu.VMEM)),
        scratch_shapes=[
            vmem((4, 512, 256), BF), vmem((4, 2, 128, 256), BF), vmem((4, 2, 128, 1024), BF),
            vmem((18, 256, 256), BF), vmem((2, 1024, 256), BF),
            vmem((128, 512), BF), vmem((480, 640), BF), vmem((2, 128, 128), BF),
            vmem((512, 512), BF), vmem((2048, 512), BF), vmem((512, 256), BF), vmem((512, 256), BF),
            vmem((128, 256), BF), vmem((4, 480, 256), F32), vmem((3, 4, 160, 256), BF),
            vmem((512, 256), F32), vmem((2, 4, 128, 256), BF), vmem((2, 4, 128, 256), BF),
            vmem((4, 2, 128, 1024), BF),
            vmem((6656, 256), F32), vmem((16, CHUNK, 128), BF), vmem((16, CHUNK, 128), BF),
            vmem((16, CHUNK, 128), F32), vmem((8, 4, 208, 128), F32), vmem((8, 4, 208, 128), BF),
            vmem((8, 3, 208, 128), BF), vmem((8, 208, 128), F32), vmem((4, CHUNK, 128), F32),
            vmem((4, CHUNK, 128), BF), vmem((3, CHUNK, 128), BF), vmem((432, 128), F32),
            vmem((16, 32, 128), BF), vmem((8, 2, 32, 128), BF),
            dma((8,)), dma((8,)), dma((8,)), dma((8,)), dma((8,)), dma((16,)), dma((16,)),
            dma((8, 4)), dma((8, 3)), dma((3,)), dma((3,)), dma((16,)), dma((8, 2)), dma,
        ],
        compiler_params=pltpu.CompilerParams(
            collective_id=0, has_side_effects=True, vmem_limit_bytes=56 * 2**20
        ),
        cost_estimate=pl.CostEstimate(flops=3_500_000_000, bytes_accessed=11_000_000, transcendentals=0),
        name="head_backward",
    )(
        cotangent.reshape(4, 512, 256),
        saved.reshape(4, 2, 128, 256),
        features,
        conv_weight.reshape(18, 256, 256),
        proj_weight,
        send,
        take,
        order,
    )


def solution(mesh):
    in_specs = (
        P("dp", None, "tile", None),
        P(),
        P(),
        P("dp", None, "tile", None, None),
        P("dp", "tile", None, None),
    )
    out_specs = (P("dp", None, "tile", None), P(("dp", "tile"), None))
    return jax.shard_map(
        per_device, mesh=mesh, in_specs=in_specs, out_specs=out_specs, check_vma=False
    )
```

```python
import math

import jax
import jax.numpy as jnp
import ml_dtypes
import numpy as np
from jax import lax
from jax.experimental import pallas as pl
from jax.experimental.pallas import tpu as pltpu
from jax.sharding import PartitionSpec as P

MESH = pl.DeviceIdType.MESH
BF = jnp.bfloat16
F32 = jnp.float32

DIRS = ((-1, 0), (1, 0), (0, -1), (0, 1), (-1, -1), (-1, 1), (1, -1), (1, 1))
MAIN = (32, 32, 16, 16, 0, 0, 0, 0)
SIZE = tuple(4 * m + 16 for m in MAIN)
START = tuple(sum(SIZE[:d]) for d in range(8))
MAIN_AT = (0, 32, 64, 80)

CHUNK = 416
HEAD_ROWS = 26


def weight(cell, fine, cells, first, last):
    at = fine - 2 * cell
    value = 0.75 if at in (0, 1) else 0.25 if at in (-1, 2) else 0.0
    if first and cell == 0 and fine == 0:
        value += 0.25
    if last and cell == cells - 1 and fine == 2 * cells - 1:
        value += 0.25
    return value


def halo_cells(d):
    dr, dc = DIRS[d]
    rows = {1: [-1, 0], -1: [8, 7], 0: list(range(8))}[dr]
    cols = {1: [-1, 0], -1: [16, 15], 0: list(range(16))}[dc]
    if dr and dc:
        return [], [(j, w) for j in rows for w in cols]
    main = [(j, w) for j in rows for w in cols]
    if dr:
        corner = [(j, w) for j in rows for w in (-1, 16)]
    else:
        corner = [(j, w) for j in (-1, 8) for w in cols]
    return main, corner


def tables():
    send = np.zeros((9, 128, 512), np.float32)
    take = np.zeros((9, 480, 640), np.float32)
    for place in range(9):
        top, bottom = place // 3 == 0, place // 3 == 2
        left, right = place % 3 == 0, place % 3 == 2
        row_w = np.array([[weight(j, r, 8, top, bottom) for r in range(16)] for j in range(-1, 9)])
        col_w = np.array([[weight(w, c, 16, left, right) for c in range(32)] for w in range(-1, 17)])

        def line(j, w):
            return np.outer(row_w[j + 1], col_w[w + 1]).reshape(512)

        for d, (dr, dc) in enumerate(DIRS):
            main, corner = halo_cells(d)
            for m, (j, w) in enumerate(main):
                send[place, MAIN_AT[d] + m] = line(j + 8 * dr, w + 16 * dc)
            for m, (j, w) in enumerate(corner):
                send[place, 96 + 4 * d + m] = line(j + 8 * dr, w + 16 * dc)

        def outside(j, w):
            return (j < 0 and top) or (j > 7 and bottom) or (w < 0 and left) or (w > 15 and right)

        for shift in range(3):
            for jr in range(10):
                for ww in range(16):
                    j, w = jr - 1, shift + ww - 1
                    if not outside(j, w):
                        take[place, shift * 160 + jr * 16 + ww, :512] = line(j, w)
            for d in range(8):
                main, corner = halo_cells(d)
                at = [(512 + MAIN_AT[d] + m, cell) for m, cell in enumerate(main)] if main else []
                at += [(608 + 4 * d + m, cell) for m, cell in enumerate(corner)]
                for column, (j, w) in at:
                    ww = w + 1 - shift
                    if 0 <= ww < 16 and not outside(j, w):
                        take[place, shift * 160 + (j + 1) * 16 + ww, column] = 1.0
    order = np.zeros((128, 128), np.float32)
    for i in range(4):
        for d in range(8):
            for cell in range(4):
                order[d * 16 + i * 4 + cell, i * 32 + d * 4 + cell] = 1.0
    as_bf16 = [a.astype(ml_dtypes.bfloat16) for a in (send, take, np.stack([order, order.T]))]
    return as_bf16


def mm(a, b):
    return jnp.dot(a, b, preferred_element_type=F32)


def mm_t(a, b):
    return lax.dot_general(a, b, (((1,), (1,)), ((), ())), preferred_element_type=F32)


def kernel(
    cot_hbm, saved_hbm, feat_hbm, w_hbm, send_hbm, take_hbm, order_hbm,
    tok_out, head_out,
    cot, saved, feat, wconv, send_m, take_m, order_m,
    saved_t, feat_t, halo_out, halo_in, corner, acc, pooled, grad_acc, grad, tok,
    head, send_c, recv_c, part, split_1, send_1, recv_1, split_2, send_2, recv_2, kept, last, send_3, recv_3,
    load_sem, halo_ss, halo_rs, tok_ss, tok_rs, c_ss, c_rs, ss_1, rs_1, ss_2, rs_2, ss_3, rs_3, out_sem,
):
    dp = lax.axis_index("dp")
    tile = lax.axis_index("tile")
    z, y, xh, core = tile // 16, (tile // 4) % 4, (tile // 2) % 2, tile % 2
    x = xh * 2 + dp
    g, row = tile % 8, tile // 8
    g0, g1, g2 = g % 2, (g // 2) % 2, g // 4
    col = g2 * 4 + (g2 + g1) % 2 * 2 + (g2 + g1 + g0) % 2
    a = jnp.where(core == 0, x, y)
    b = jnp.where(core == 0, y, x)

    def gray(c):
        c0, c1, c2 = c % 2, (c // 2) % 2, c // 4
        return c2 * 4 + (c2 + c1) % 2 * 2 + (c1 + c0) % 2

    def in_plane(to_a, to_b):
        to_x = jnp.where(core == 0, to_a, to_b)
        to_y = jnp.where(core == 0, to_b, to_a)
        return {"dp": to_x % 2, "tile": z * 16 + to_y * 4 + to_x // 2 * 2 + core}

    def remote(src, dst, send_sem, recv_sem, device):
        return pltpu.make_async_remote_copy(
            src_ref=src, dst_ref=dst, send_sem=send_sem, recv_sem=recv_sem,
            device_id=device, device_id_type=MESH,
        )

    place = (
        jnp.where(row == 0, 0, jnp.where(row == 15, 2, 1)) * 3
        + jnp.where(col == 0, 0, jnp.where(col == 7, 2, 1))
    )
    loads = [
        pltpu.make_async_copy(src, dst, load_sem.at[n])
        for n, (src, dst) in enumerate([
            (cot_hbm, cot), (send_hbm.at[place], send_m), (order_hbm, order_m),
            (take_hbm.at[place], take_m), (saved_hbm, saved), (w_hbm, wconv), (feat_hbm, feat),
        ])
    ]
    for load in loads:
        load.start()

    barrier = pltpu.get_barrier_semaphore()

    def greet(device):
        pl.semaphore_signal(barrier, inc=1, device_id=device, device_id_type=MESH)

    def has(dr, dc):
        to_row, to_col = row + dr, col + dc
        ok = jnp.logical_and(to_row >= 0, to_row < 16)
        return jnp.logical_and(ok, jnp.logical_and(to_col >= 0, to_col < 8))

    def beside(dr, dc):
        return jnp.clip(row + dr, 0, 15) * 8 + gray(jnp.clip(col + dc, 0, 7))

    greeted = jnp.int32(0)
    for dr, dc in DIRS:
        if dr:

            @pl.when(has(dr, dc))
            def _():
                greet({"tile": beside(dr, dc)})

            greeted = greeted + has(dr, dc).astype(jnp.int32)
    for n in range(1, 8):
        greet({"tile": row * 8 + (g + n) % 8})
    for n in range(2):
        greet({"dp": 1 - dp, "tile": z * 16 + y * 4 + n * 2 + core})
        greet({"tile": z * 16 + (y // 2 * 2 + 2 + n) % 4 * 4 + xh * 2 + core})
    for n in range(1, 8):
        for c in range(2):
            greet({"tile": (z + n) % 8 * 16 + y * 4 + xh * 2 + c})
    greeted = greeted + 25

    for n in range(3):
        loads[n].wait()
    for i in range(4):
        r = mm(send_m[...], cot[i]).astype(BF)
        for d in range(4):
            m = MAIN[d]
            halo_out[START[d] + i * m : START[d] + (i + 1) * m, :] = r[MAIN_AT[d] : MAIN_AT[d] + m]
        corner[i * 32 : (i + 1) * 32, :] = r[96:128]
    corners = mm(order_m[0], corner[...]).astype(BF)
    for d in range(8):
        halo_out[START[d] + 4 * MAIN[d] : START[d] + SIZE[d], :] = corners[d * 16 : d * 16 + 16]

    def halo(d):
        return remote(
            halo_out.at[START[d] : START[d] + SIZE[d]], halo_in.at[START[d] : START[d] + SIZE[d]],
            halo_ss.at[d], halo_rs.at[d], {"tile": beside(*DIRS[d])},
        )

    pl.semaphore_wait(barrier, greeted)
    for d in range(8):
        dr, dc = DIRS[d]

        @pl.when(has(dr, dc))
        def _():
            halo(d).start()

        @pl.when(jnp.logical_not(has(-dr, -dc)))
        def _():
            halo_in[START[d] : START[d] + SIZE[d], :] = jnp.zeros((SIZE[d], 256), BF)

    loads[3].wait()
    for i in range(4):
        acc[i] = mm(take_m[:, :512], cot[i])
    loads[4].wait()
    for k in range(2):
        for i in range(4):
            saved_t[k * 256 : (k + 1) * 256, i * 128 : (i + 1) * 128] = saved[i, k].T

    for d in range(8):
        dr, dc = DIRS[d]

        @pl.when(has(-dr, -dc))
        def _():
            halo(d).wait_recv()

    for d in range(8):
        at = START[d] + 4 * MAIN[d]
        corner[d * 16 : d * 16 + 16, :] = halo_in[at : at + 16, :]
    corners = mm(order_m[1], corner[...]).astype(BF)
    for i in range(4):
        parts = [halo_in[START[d] + i * MAIN[d] : START[d] + (i + 1) * MAIN[d], :] for d in range(4)]
        ring = jnp.concatenate(parts + [corners[i * 32 : (i + 1) * 32]], axis=0)
        full = (acc[i] + mm(take_m[:, 512:], ring)).astype(BF)
        for shift in range(3):
            pooled[shift, i] = full[shift * 160 : (shift + 1) * 160]

    def tap(t):
        u, v = t // 3, t % 3
        return pooled[2 - v, :, (2 - u) * 16 : (2 - u) * 16 + 128, :].reshape(512, 256)

    def regroup(k, n):
        there = (g + n) % 8
        return remote(
            grad.at[k, :, pl.ds(pl.multiple_of(there * 16, 16), 16)],
            tok.at[k, :, pl.ds(pl.multiple_of(col * 16, 16), 16)],
            tok_ss.at[k, n], tok_rs.at[k, n], {"tile": row * 8 + there},
        )

    loads[5].wait()
    for k in (1, 0):
        for t in range(9):
            term = mm_t(tap(t), wconv[k * 9 + t])
            if t == 0:
                grad_acc[...] = term
            elif t < 8:
                grad_acc[...] += term
            else:
                grad[k] = (grad_acc[...] + term).astype(BF).reshape(4, 128, 256)
        for n in range(1, 8):
            regroup(k, n).start()
        tok[k, :, pl.ds(pl.multiple_of(col * 16, 16), 16)] = grad[k, :, pl.ds(pl.multiple_of(g * 16, 16), 16)]

    mine = pl.ds(pl.multiple_of(core * 128, 128), 128)
    theirs = pl.ds(pl.multiple_of((1 - core) * 128, 128), 128)
    pair_device = {"tile": tile + 1 - 2 * core}

    def swap(q):
        return remote(send_c.at[q], recv_c.at[q], c_ss.at[q], c_rs.at[q], pair_device)

    def to_first(pair, n):
        return jnp.where(core == 0, pair // 4 + n % 2 * 2, n)

    def first(pair, n):
        to_a = to_first(pair, n)
        slot = jnp.where(core == 0, pair % 4 * 2 + n // 2, pair)
        step = (to_a - a + 3) % 4
        return remote(
            send_1.at[pair, n], recv_1.at[slot, step], ss_1.at[pair, n], rs_1.at[slot, step], in_plane(to_a, b)
        )

    def ready(q):
        send_c[q] = head[q * CHUNK : (q + 1) * CHUNK, theirs].astype(BF)
        swap(q).start()

    def reduced(pair):
        for q in (2 * pair, 2 * pair + 1):
            swap(q).wait_recv()
            part[q] = head[q * CHUNK : (q + 1) * CHUNK, mine] + recv_c[q].astype(F32)

        @pl.when(core == 0)
        def _():
            for n in range(4):
                for p in range(4):
                    at = p * 104 + n % 2 * 52
                    split_1[pair, n, p * 52 : p * 52 + 52, :] = part[2 * pair + n // 2, at : at + 52, :]

        @pl.when(core == 1)
        def _():
            for n in range(4):
                for h in range(2):
                    split_1[pair, n, h * 104 : h * 104 + 104, :] = part[2 * pair + h, n * 104 : n * 104 + 104, :]

        for n in range(4):
            send_1[pair, n] = split_1[pair, n].astype(BF)

            @pl.when(a != to_first(pair, n))
            def _():
                first(pair, n).start()

    def second(j, to_b):
        step = (to_b - b + 3) % 4
        return remote(
            send_2.at[j, to_b], recv_2.at[j, step], ss_2.at[j, to_b], rs_2.at[j, step], in_plane(a, to_b)
        )

    def to_second(j):
        for h in range(2):
            e = jnp.where(core == 0, 2 * j + h, j + 4 * h)
            pair = jnp.where(core == 0, a % 2 * 4 + j, e)
            n = jnp.where(core == 0, h * 2 + a // 2, a)
            total = split_1[pair, n]
            for s in range(3):
                remote(
                    send_1.at[0, 0], recv_1.at[e, s], ss_1.at[0, 0], rs_1.at[e, s], pair_device
                ).wait_recv()
                total = total + recv_1[e, s].astype(F32)
            kept[j, h] = total

        @pl.when(core == 0)
        def _():
            for to_b in range(4):
                for h in range(2):
                    split_2[j, to_b, h * 52 : h * 52 + 52, :] = kept[j, h, to_b * 52 : to_b * 52 + 52, :]

        @pl.when(core == 1)
        def _():
            for to_b in range(4):
                for h in range(2):
                    at = h * 104 + to_b // 2 * 52
                    split_2[j, to_b, h * 52 : h * 52 + 52, :] = kept[j, to_b % 2, at : at + 52, :]

        for to_b in range(4):
            split_2[j, to_b, 104:112, :] = jnp.zeros((8, 128), F32)
            send_2[j, to_b] = split_2[j, to_b].astype(BF)

            @pl.when(b != to_b)
            def _():
                second(j, to_b).start()

    def third(p):
        return remote(
            send_3.at[p], recv_3.at[z, core], ss_3.at[p], rs_3.at[z, core],
            {"tile": p // 2 * 16 + y * 4 + xh * 2 + p % 2},
        )

    def to_self(p):
        return jnp.logical_and(z == p // 2, core == p % 2)

    def to_third(j):
        total = split_2[j, b]
        for s in range(3):
            second(j, (b + s + 1) % 4).wait_recv()
            total = total + recv_2[j, s].astype(F32)
        last[j] = total
        for n in range(4):
            p = 4 * j + n
            send_3[p] = last[j, n * HEAD_ROWS : n * HEAD_ROWS + 32, :].astype(BF)

            @pl.when(jnp.logical_not(to_self(p)))
            def _():
                third(p).start()

            @pl.when(to_self(p))
            def _():
                recv_3[z, core] = send_3[p]

    for k in (1, 0):
        for t in range(9):
            at = 2048 + (k * 9 + t) * 256
            head[at : at + 256, :] = mm(saved_t[k * 256 : (k + 1) * 256, :], tap(t))
        for q in (range(5, 11), range(11, 16))[k]:
            ready(q)
    loads[6].wait()
    for k in range(2):
        for i in range(4):
            feat_t[k * 1024 : (k + 1) * 1024, i * 128 : (i + 1) * 128] = feat[i, k].T
    for pair in (7, 3, 6, 5, 4):
        reduced(pair)

    for k in (1, 0):
        for n in range(1, 8):
            regroup(k, n).wait_recv()
        for h in range(4):
            at = k * 1024 + h * 256
            head[at : at + 256, :] = mm(feat_t[at : at + 256, :], tok[k].reshape(512, 256))
        for q in (range(0, 3), range(3, 5))[k]:
            ready(q)
    out_copy = pltpu.make_async_copy(tok, tok_out, out_sem)
    out_copy.start()
    reduced(2)
    to_second(3)
    reduced(1)
    reduced(0)
    to_third(3)
    to_second(2)
    to_second(1)
    to_third(2)
    to_second(0)
    to_third(1)
    to_third(0)

    for c in range(2):
        total = jnp.zeros((32, 128), F32)
        for zz in range(8):

            @pl.when(jnp.logical_not(to_self(zz * 2 + c)))
            def _():
                remote(
                    send_3.at[0], recv_3.at[zz, c], ss_3.at[0], rs_3.at[zz, c], pair_device
                ).wait_recv()

            total = total + recv_3[zz, c].astype(F32)
        head_out[:, c * 128 : (c + 1) * 128] = total[:HEAD_ROWS]

    for d in range(8):

        @pl.when(has(*DIRS[d]))
        def _():
            halo(d).wait_send()

    for k in range(2):
        for n in range(1, 8):
            regroup(k, n).wait_send()
    for q in range(16):
        swap(q).wait_send()
    for pair in range(8):
        for n in range(4):

            @pl.when(a != to_first(pair, n))
            def _():
                first(pair, n).wait_send()

    for j in range(4):
        for to_b in range(4):

            @pl.when(b != to_b)
            def _():
                second(j, to_b).wait_send()

    for p in range(16):

        @pl.when(jnp.logical_not(to_self(p)))
        def _():
            third(p).wait_send()

    out_copy.wait()


def finish(tok_hbm, proj_hbm, head_in, fg_hbm, head_out, tok, proj, fg, load_sem, out_sem):
    loads = [
        pltpu.make_async_copy(src.at[k], dst.at[k], load_sem.at[2 * n + k])
        for k in range(2)
        for n, (src, dst) in enumerate([(tok_hbm, tok), (proj_hbm, proj)])
    ]
    for load in loads:
        load.start()
    head_out[...] = head_in[...] * (1.0 / math.sqrt(8 * 16384))
    outs = []
    for k in range(2):
        loads[2 * k].wait()
        loads[2 * k + 1].wait()
        for i in range(4):
            fg[i, k] = mm_t(tok[k, i], proj[k]).astype(BF)
            outs.append(pltpu.make_async_copy(fg.at[i, k], fg_hbm.at[i, k], out_sem.at[i, k]))
            outs[-1].start()
    for out in outs:
        out.wait()


def per_device(features, proj_weight, conv_weight, saved, cotangent):
    send, take, order = (jnp.asarray(t) for t in tables())
    hbm = pl.BlockSpec(memory_space=pl.ANY)
    whole = pl.BlockSpec(memory_space=pltpu.VMEM)
    dma = pltpu.SemaphoreType.DMA
    vmem = pltpu.VMEM
    tok, head = pl.pallas_call(
        kernel,
        out_shape=(
            jax.ShapeDtypeStruct((2, 4, 128, 256), BF),
            jax.ShapeDtypeStruct((HEAD_ROWS, 256), F32),
        ),
        in_specs=[hbm] * 7,
        out_specs=(hbm, whole),
        scratch_shapes=[
            vmem((4, 512, 256), BF), vmem((4, 2, 128, 256), BF), vmem((4, 2, 128, 1024), BF),
            vmem((18, 256, 256), BF),
            vmem((128, 512), BF), vmem((480, 640), BF), vmem((2, 128, 128), BF),
            vmem((512, 512), BF), vmem((2048, 512), BF), vmem((512, 256), BF), vmem((512, 256), BF),
            vmem((128, 256), BF), vmem((4, 480, 256), F32), vmem((3, 4, 160, 256), BF),
            vmem((512, 256), F32), vmem((2, 4, 128, 256), BF), vmem((2, 4, 128, 256), BF),
            vmem((6656, 256), F32), vmem((16, CHUNK, 128), BF), vmem((16, CHUNK, 128), BF),
            vmem((16, CHUNK, 128), F32), vmem((8, 4, 208, 128), F32), vmem((8, 4, 208, 128), BF),
            vmem((8, 3, 208, 128), BF), vmem((4, 4, 112, 128), F32), vmem((4, 4, 112, 128), BF),
            vmem((4, 3, 112, 128), BF), vmem((4, 2, 208, 128), F32), vmem((4, 112, 128), F32),
            vmem((16, 32, 128), BF), vmem((8, 2, 32, 128), BF),
            dma((7,)), dma((8,)), dma((8,)), dma((2, 8)), dma((2, 8)), dma((16,)), dma((16,)),
            dma((8, 4)), dma((8, 3)), dma((4, 4)), dma((4, 3)), dma((16,)), dma((8, 2)), dma,
        ],
        compiler_params=pltpu.CompilerParams(
            collective_id=0, has_side_effects=True, vmem_limit_bytes=56 * 2**20
        ),
        cost_estimate=pl.CostEstimate(flops=3_000_000_000, bytes_accessed=9_000_000, transcendentals=0),
        name="head_backward",
    )(
        cotangent.reshape(4, 512, 256),
        saved.reshape(4, 2, 128, 256),
        features,
        conv_weight.reshape(18, 256, 256),
        send,
        take,
        order,
    )
    return pl.pallas_call(
        finish,
        out_shape=(
            jax.ShapeDtypeStruct((4, 2, 128, 1024), BF),
            jax.ShapeDtypeStruct((HEAD_ROWS, 256), F32),
        ),
        in_specs=[hbm, hbm, whole],
        out_specs=(hbm, whole),
        scratch_shapes=[
            vmem((2, 4, 128, 256), BF), vmem((2, 1024, 256), BF), vmem((4, 2, 128, 1024), BF),
            dma((4,)), dma((4, 2)),
        ],
        compiler_params=pltpu.CompilerParams(vmem_limit_bytes=62 * 2**20),
        cost_estimate=pl.CostEstimate(flops=540_000_000, bytes_accessed=3_600_000, transcendentals=0),
        name="feature_grad",
    )(tok, proj_weight, head)


def solution(mesh):
    in_specs = (
        P("dp", None, "tile", None),
        P(),
        P(),
        P("dp", None, "tile", None, None),
        P("dp", "tile", None, None),
    )
    out_specs = (P("dp", None, "tile", None), P(("dp", "tile"), None))
    return jax.shard_map(
        per_device, mesh=mesh, in_specs=in_specs, out_specs=out_specs, check_vma=False
    )
```

```python
import math

import jax
import jax.numpy as jnp
import ml_dtypes
import numpy as np
from jax import lax
from jax.experimental import pallas as pl
from jax.experimental.pallas import tpu as pltpu
from jax.sharding import PartitionSpec as P

MESH = pl.DeviceIdType.MESH
BF = jnp.bfloat16
F32 = jnp.float32

DIRS = ((-1, 0), (1, 0), (0, -1), (0, 1), (-1, -1), (-1, 1), (1, -1), (1, 1))
MAIN = (32, 32, 16, 16, 0, 0, 0, 0)
SIZE = tuple(4 * m + 16 for m in MAIN)
START = tuple(sum(SIZE[:d]) for d in range(8))
MAIN_AT = (0, 32, 64, 80)

CHUNK = 416
HEAD_ROWS = 26


def weight(cell, fine, cells, first, last):
    at = fine - 2 * cell
    value = 0.75 if at in (0, 1) else 0.25 if at in (-1, 2) else 0.0
    if first and cell == 0 and fine == 0:
        value += 0.25
    if last and cell == cells - 1 and fine == 2 * cells - 1:
        value += 0.25
    return value


def halo_cells(d):
    dr, dc = DIRS[d]
    rows = {1: [-1, 0], -1: [8, 7], 0: list(range(8))}[dr]
    cols = {1: [-1, 0], -1: [16, 15], 0: list(range(16))}[dc]
    if dr and dc:
        return [], [(j, w) for j in rows for w in cols]
    main = [(j, w) for j in rows for w in cols]
    if dr:
        corner = [(j, w) for j in rows for w in (-1, 16)]
    else:
        corner = [(j, w) for j in (-1, 8) for w in cols]
    return main, corner


def tables():
    send = np.zeros((9, 128, 512), np.float32)
    take = np.zeros((9, 480, 640), np.float32)
    for place in range(9):
        top, bottom = place // 3 == 0, place // 3 == 2
        left, right = place % 3 == 0, place % 3 == 2
        row_w = np.array([[weight(j, r, 8, top, bottom) for r in range(16)] for j in range(-1, 9)])
        col_w = np.array([[weight(w, c, 16, left, right) for c in range(32)] for w in range(-1, 17)])

        def line(j, w):
            return np.outer(row_w[j + 1], col_w[w + 1]).reshape(512)

        for d, (dr, dc) in enumerate(DIRS):
            main, corner = halo_cells(d)
            for m, (j, w) in enumerate(main):
                send[place, MAIN_AT[d] + m] = line(j + 8 * dr, w + 16 * dc)
            for m, (j, w) in enumerate(corner):
                send[place, 96 + 4 * d + m] = line(j + 8 * dr, w + 16 * dc)

        def outside(j, w):
            return (j < 0 and top) or (j > 7 and bottom) or (w < 0 and left) or (w > 15 and right)

        for shift in range(3):
            for jr in range(10):
                for ww in range(16):
                    j, w = jr - 1, shift + ww - 1
                    if not outside(j, w):
                        take[place, shift * 160 + jr * 16 + ww, :512] = line(j, w)
            for d in range(8):
                main, corner = halo_cells(d)
                at = [(512 + MAIN_AT[d] + m, cell) for m, cell in enumerate(main)] if main else []
                at += [(608 + 4 * d + m, cell) for m, cell in enumerate(corner)]
                for column, (j, w) in at:
                    ww = w + 1 - shift
                    if 0 <= ww < 16 and not outside(j, w):
                        take[place, shift * 160 + (j + 1) * 16 + ww, column] = 1.0
    order = np.zeros((128, 128), np.float32)
    for i in range(4):
        for d in range(8):
            for cell in range(4):
                order[d * 16 + i * 4 + cell, i * 32 + d * 4 + cell] = 1.0
    as_bf16 = [a.astype(ml_dtypes.bfloat16) for a in (send, take, np.stack([order, order.T]))]
    return as_bf16


def mm(a, b):
    return jnp.dot(a, b, preferred_element_type=F32)


def mm_t(a, b):
    return lax.dot_general(a, b, (((1,), (1,)), ((), ())), preferred_element_type=F32)


def kernel(
    cot_hbm, saved_hbm, feat_hbm, w_hbm, proj_hbm, send_hbm, take_hbm, order_hbm,
    fg_out, head_out,
    cot, saved, feat, wconv, proj, send_m, take_m, order_m,
    saved_t, feat_t, halo_out, halo_in, corner, acc, pooled, grad_acc, grad, tok, fg,
    head, send_c, recv_c, part, split_1, send_1, recv_1, split_2, send_2, recv_2, kept, last, send_3, recv_3,
    load_sem, halo_ss, halo_rs, tok_ss, tok_rs, c_ss, c_rs, ss_1, rs_1, ss_2, rs_2, ss_3, rs_3, out_sem,
):
    dp = lax.axis_index("dp")
    tile = lax.axis_index("tile")
    z, y, xh, core = tile // 16, (tile // 4) % 4, (tile // 2) % 2, tile % 2
    x = xh * 2 + dp
    g, row = tile % 8, tile // 8
    g0, g1, g2 = g % 2, (g // 2) % 2, g // 4
    col = g2 * 4 + (g2 + g1) % 2 * 2 + (g2 + g1 + g0) % 2
    a = jnp.where(core == 0, x, y)
    b = jnp.where(core == 0, y, x)

    def gray(c):
        c0, c1, c2 = c % 2, (c // 2) % 2, c // 4
        return c2 * 4 + (c2 + c1) % 2 * 2 + (c1 + c0) % 2

    def in_plane(to_a, to_b):
        to_x = jnp.where(core == 0, to_a, to_b)
        to_y = jnp.where(core == 0, to_b, to_a)
        return {"dp": to_x % 2, "tile": z * 16 + to_y * 4 + to_x // 2 * 2 + core}

    def remote(src, dst, send_sem, recv_sem, device):
        return pltpu.make_async_remote_copy(
            src_ref=src, dst_ref=dst, send_sem=send_sem, recv_sem=recv_sem,
            device_id=device, device_id_type=MESH,
        )

    place = (
        jnp.where(row == 0, 0, jnp.where(row == 15, 2, 1)) * 3
        + jnp.where(col == 0, 0, jnp.where(col == 7, 2, 1))
    )
    loads = [
        pltpu.make_async_copy(src, dst, load_sem.at[n])
        for n, (src, dst) in enumerate([
            (cot_hbm, cot), (send_hbm.at[place], send_m), (order_hbm, order_m),
            (take_hbm.at[place], take_m), (saved_hbm, saved), (w_hbm, wconv), (feat_hbm, feat),
            (proj_hbm, proj),
        ])
    ]
    for load in loads[:4]:
        load.start()

    barrier = pltpu.get_barrier_semaphore()

    def greet(device):
        pl.semaphore_signal(barrier, inc=1, device_id=device, device_id_type=MESH)

    def has(dr, dc):
        to_row, to_col = row + dr, col + dc
        ok = jnp.logical_and(to_row >= 0, to_row < 16)
        return jnp.logical_and(ok, jnp.logical_and(to_col >= 0, to_col < 8))

    def beside(dr, dc):
        return jnp.clip(row + dr, 0, 15) * 8 + gray(jnp.clip(col + dc, 0, 7))

    greeted = jnp.int32(0)
    for dr, dc in DIRS:
        if dr:

            @pl.when(has(dr, dc))
            def _():
                greet({"tile": beside(dr, dc)})

            greeted = greeted + has(dr, dc).astype(jnp.int32)
    for n in range(1, 8):
        greet({"tile": row * 8 + (g + n) % 8})
    for n in range(2):
        greet({"dp": 1 - dp, "tile": z * 16 + y * 4 + n * 2 + core})
        greet({"tile": z * 16 + (y // 2 * 2 + 2 + n) % 4 * 4 + xh * 2 + core})
    for n in range(1, 8):
        for c in range(2):
            greet({"tile": (z + n) % 8 * 16 + y * 4 + xh * 2 + c})
    greeted = greeted + 25

    for n in range(3):
        loads[n].wait()
    for load in loads[4:]:
        load.start()
    for i in range(4):
        r = mm(send_m[...], cot[i]).astype(BF)
        for d in range(4):
            m = MAIN[d]
            halo_out[START[d] + i * m : START[d] + (i + 1) * m, :] = r[MAIN_AT[d] : MAIN_AT[d] + m]
        corner[i * 32 : (i + 1) * 32, :] = r[96:128]
    corners = mm(order_m[0], corner[...]).astype(BF)
    for d in range(8):
        halo_out[START[d] + 4 * MAIN[d] : START[d] + SIZE[d], :] = corners[d * 16 : d * 16 + 16]

    def halo(d):
        return remote(
            halo_out.at[START[d] : START[d] + SIZE[d]], halo_in.at[START[d] : START[d] + SIZE[d]],
            halo_ss.at[d], halo_rs.at[d], {"tile": beside(*DIRS[d])},
        )

    pl.semaphore_wait(barrier, greeted)
    for d in range(8):
        dr, dc = DIRS[d]

        @pl.when(has(dr, dc))
        def _():
            halo(d).start()

        @pl.when(jnp.logical_not(has(-dr, -dc)))
        def _():
            halo_in[START[d] : START[d] + SIZE[d], :] = jnp.zeros((SIZE[d], 256), BF)

    loads[3].wait()
    for i in range(4):
        acc[i] = mm(take_m[:, :512], cot[i])
    loads[4].wait()
    for k in range(2):
        for i in range(4):
            saved_t[k * 256 : (k + 1) * 256, i * 128 : (i + 1) * 128] = saved[i, k].T

    for d in range(8):
        dr, dc = DIRS[d]

        @pl.when(has(-dr, -dc))
        def _():
            halo(d).wait_recv()

    for d in range(8):
        at = START[d] + 4 * MAIN[d]
        corner[d * 16 : d * 16 + 16, :] = halo_in[at : at + 16, :]
    corners = mm(order_m[1], corner[...]).astype(BF)
    for i in range(4):
        parts = [halo_in[START[d] + i * MAIN[d] : START[d] + (i + 1) * MAIN[d], :] for d in range(4)]
        ring = jnp.concatenate(parts + [corners[i * 32 : (i + 1) * 32]], axis=0)
        full = (acc[i] + mm(take_m[:, 512:], ring)).astype(BF)
        for shift in range(3):
            pooled[shift, i] = full[shift * 160 : (shift + 1) * 160]

    def tap(t):
        u, v = t // 3, t % 3
        return pooled[2 - v, :, (2 - u) * 16 : (2 - u) * 16 + 128, :].reshape(512, 256)

    def regroup(k, n):
        there = (g + n) % 8
        return remote(
            grad.at[k, :, pl.ds(pl.multiple_of(there * 16, 16), 16)],
            tok.at[k, :, pl.ds(pl.multiple_of(col * 16, 16), 16)],
            tok_ss.at[k, n], tok_rs.at[k, n], {"tile": row * 8 + there},
        )

    loads[5].wait()
    for k in range(2):
        for t in range(9):
            term = mm_t(tap(t), wconv[k * 9 + t])
            if t == 0:
                grad_acc[...] = term
            elif t < 8:
                grad_acc[...] += term
            else:
                grad[k] = (grad_acc[...] + term).astype(BF).reshape(4, 128, 256)
        for n in range(1, 8):
            regroup(k, n).start()
        tok[k, :, pl.ds(pl.multiple_of(col * 16, 16), 16)] = grad[k, :, pl.ds(pl.multiple_of(g * 16, 16), 16)]

    mine = pl.ds(pl.multiple_of(core * 128, 128), 128)
    theirs = pl.ds(pl.multiple_of((1 - core) * 128, 128), 128)
    pair_device = {"tile": tile + 1 - 2 * core}

    def swap(q):
        return remote(send_c.at[q], recv_c.at[q], c_ss.at[q], c_rs.at[q], pair_device)

    def to_first(pair, n):
        return jnp.where(core == 0, pair // 4 + n % 2 * 2, n)

    def first(pair, n):
        to_a = to_first(pair, n)
        slot = jnp.where(core == 0, pair % 4 * 2 + n // 2, pair)
        step = (to_a - a + 3) % 4
        return remote(
            send_1.at[pair, n], recv_1.at[slot, step], ss_1.at[pair, n], rs_1.at[slot, step], in_plane(to_a, b)
        )

    def ready(q):
        send_c[q] = head[q * CHUNK : (q + 1) * CHUNK, theirs].astype(BF)
        swap(q).start()

    def reduced(pair):
        for q in (2 * pair, 2 * pair + 1):
            swap(q).wait_recv()
            part[q] = head[q * CHUNK : (q + 1) * CHUNK, mine] + recv_c[q].astype(F32)

        @pl.when(core == 0)
        def _():
            for n in range(4):
                for p in range(4):
                    at = p * 104 + n % 2 * 52
                    split_1[pair, n, p * 52 : p * 52 + 52, :] = part[2 * pair + n // 2, at : at + 52, :]

        @pl.when(core == 1)
        def _():
            for n in range(4):
                for h in range(2):
                    split_1[pair, n, h * 104 : h * 104 + 104, :] = part[2 * pair + h, n * 104 : n * 104 + 104, :]

        for n in range(4):
            send_1[pair, n] = split_1[pair, n].astype(BF)

            @pl.when(a != to_first(pair, n))
            def _():
                first(pair, n).start()

    def second(j, to_b):
        step = (to_b - b + 3) % 4
        return remote(
            send_2.at[j, to_b], recv_2.at[j, step], ss_2.at[j, to_b], rs_2.at[j, step], in_plane(a, to_b)
        )

    def to_second(j):
        for h in range(2):
            e = jnp.where(core == 0, 2 * j + h, j + 4 * h)
            pair = jnp.where(core == 0, a % 2 * 4 + j, e)
            n = jnp.where(core == 0, h * 2 + a // 2, a)
            total = split_1[pair, n]
            for s in range(3):
                remote(
                    send_1.at[0, 0], recv_1.at[e, s], ss_1.at[0, 0], rs_1.at[e, s], pair_device
                ).wait_recv()
                total = total + recv_1[e, s].astype(F32)
            kept[j, h] = total

        @pl.when(core == 0)
        def _():
            for to_b in range(4):
                for h in range(2):
                    split_2[j, to_b, h * 52 : h * 52 + 52, :] = kept[j, h, to_b * 52 : to_b * 52 + 52, :]

        @pl.when(core == 1)
        def _():
            for to_b in range(4):
                for h in range(2):
                    at = h * 104 + to_b // 2 * 52
                    split_2[j, to_b, h * 52 : h * 52 + 52, :] = kept[j, to_b % 2, at : at + 52, :]

        for to_b in range(4):
            split_2[j, to_b, 104:112, :] = jnp.zeros((8, 128), F32)
            send_2[j, to_b] = split_2[j, to_b].astype(BF)

            @pl.when(b != to_b)
            def _():
                second(j, to_b).start()

    def third(p):
        return remote(
            send_3.at[p], recv_3.at[z, core], ss_3.at[p], rs_3.at[z, core],
            {"tile": p // 2 * 16 + y * 4 + xh * 2 + p % 2},
        )

    def to_self(p):
        return jnp.logical_and(z == p // 2, core == p % 2)

    def to_third(j):
        total = split_2[j, b]
        for s in range(3):
            second(j, (b + s + 1) % 4).wait_recv()
            total = total + recv_2[j, s].astype(F32)
        last[j] = total
        for n in range(4):
            p = 4 * j + n
            send_3[p] = last[j, n * HEAD_ROWS : n * HEAD_ROWS + 32, :].astype(BF)

            @pl.when(jnp.logical_not(to_self(p)))
            def _():
                third(p).start()

            @pl.when(to_self(p))
            def _():
                recv_3[z, core] = send_3[p]

    for k in (1, 0):
        for t in range(9):
            at = 2048 + (k * 9 + t) * 256
            head[at : at + 256, :] = mm(saved_t[k * 256 : (k + 1) * 256, :], tap(t))
        for q in (range(5, 11), range(11, 16))[k]:
            ready(q)
    loads[6].wait()
    for k in range(2):
        for i in range(4):
            feat_t[k * 1024 : (k + 1) * 1024, i * 128 : (i + 1) * 128] = feat[i, k].T
    for pair in (7, 3, 4, 5, 6):
        reduced(pair)

    for k in range(2):
        for n in range(1, 8):
            regroup(k, n).wait_recv()
        for h in range(4):
            at = k * 1024 + h * 256
            head[at : at + 256, :] = mm(feat_t[at : at + 256, :], tok[k].reshape(512, 256))
        for q in (range(0, 2), range(2, 5))[k]:
            ready(q)
    reduced(0)
    to_second(3)
    reduced(1)
    reduced(2)

    loads[7].wait()
    for k in range(2):
        tokens = tok[k].reshape(512, 256)
        for n in range(4):
            fg[:, k, :, n * 256 : n * 256 + 256] = (
                mm_t(tokens, proj[k, n * 256 : n * 256 + 256]).astype(BF).reshape(4, 128, 256)
            )
    out_copy = pltpu.make_async_copy(fg, fg_out, out_sem)
    out_copy.start()

    to_second(0)
    to_third(3)
    to_second(1)
    to_third(0)
    to_second(2)
    to_third(1)
    to_third(2)

    for c in range(2):
        total = jnp.zeros((32, 128), F32)
        for zz in range(8):

            @pl.when(jnp.logical_not(to_self(zz * 2 + c)))
            def _():
                remote(
                    send_3.at[0], recv_3.at[zz, c], ss_3.at[0], rs_3.at[zz, c], pair_device
                ).wait_recv()

            total = total + recv_3[zz, c].astype(F32)
        head_out[:, c * 128 : (c + 1) * 128] = total[:HEAD_ROWS] * (1.0 / math.sqrt(8 * 16384))

    for d in range(8):

        @pl.when(has(*DIRS[d]))
        def _():
            halo(d).wait_send()

    for k in range(2):
        for n in range(1, 8):
            regroup(k, n).wait_send()
    for q in range(16):
        swap(q).wait_send()
    for pair in range(8):
        for n in range(4):

            @pl.when(a != to_first(pair, n))
            def _():
                first(pair, n).wait_send()

    for j in range(4):
        for to_b in range(4):

            @pl.when(b != to_b)
            def _():
                second(j, to_b).wait_send()

    for p in range(16):

        @pl.when(jnp.logical_not(to_self(p)))
        def _():
            third(p).wait_send()

    out_copy.wait()


def per_device(features, proj_weight, conv_weight, saved, cotangent):
    send, take, order = (jnp.asarray(t) for t in tables())
    hbm = pl.BlockSpec(memory_space=pltpu.HBM)
    whole = pl.BlockSpec(memory_space=pltpu.VMEM)
    dma = pltpu.SemaphoreType.DMA
    vmem = pltpu.VMEM
    return pl.pallas_call(
        kernel,
        out_shape=(
            jax.ShapeDtypeStruct((4, 2, 128, 1024), BF),
            jax.ShapeDtypeStruct((HEAD_ROWS, 256), F32),
        ),
        in_specs=[hbm] * 8,
        out_specs=(pl.BlockSpec(memory_space=pl.ANY), whole),
        scratch_shapes=[
            vmem((4, 512, 256), BF), vmem((4, 2, 128, 256), BF), vmem((4, 2, 128, 1024), BF),
            vmem((18, 256, 256), BF), vmem((2, 1024, 256), BF),
            vmem((128, 512), BF), vmem((480, 640), BF), vmem((2, 128, 128), BF),
            vmem((512, 512), BF), vmem((2048, 512), BF), vmem((512, 256), BF), vmem((512, 256), BF),
            vmem((128, 256), BF), vmem((4, 480, 256), F32), vmem((3, 4, 160, 256), BF),
            vmem((512, 256), F32), vmem((2, 4, 128, 256), BF), vmem((2, 4, 128, 256), BF),
            vmem((4, 2, 128, 1024), BF),
            vmem((6656, 256), F32), vmem((16, CHUNK, 128), BF), vmem((16, CHUNK, 128), BF),
            vmem((16, CHUNK, 128), F32), vmem((8, 4, 208, 128), F32), vmem((8, 4, 208, 128), BF),
            vmem((8, 3, 208, 128), BF), vmem((4, 4, 112, 128), F32), vmem((4, 4, 112, 128), BF),
            vmem((4, 3, 112, 128), BF), vmem((4, 2, 208, 128), F32), vmem((4, 112, 128), F32),
            vmem((16, 32, 128), BF), vmem((8, 2, 32, 128), BF),
            dma((8,)), dma((8,)), dma((8,)), dma((2, 8)), dma((2, 8)), dma((16,)), dma((16,)),
            dma((8, 4)), dma((8, 3)), dma((4, 4)), dma((4, 3)), dma((16,)), dma((8, 2)), dma,
        ],
        compiler_params=pltpu.CompilerParams(
            collective_id=0, has_side_effects=True, vmem_limit_bytes=56 * 2**20
        ),
        cost_estimate=pl.CostEstimate(flops=3_000_000_000, bytes_accessed=9_000_000, transcendentals=0),
        name="head_backward",
    )(
        cotangent.reshape(4, 512, 256),
        saved.reshape(4, 2, 128, 256),
        features,
        conv_weight.reshape(18, 256, 256),
        proj_weight,
        send,
        take,
        order,
    )


def solution(mesh):
    in_specs = (
        P("dp", None, "tile", None),
        P(),
        P(),
        P("dp", None, "tile", None, None),
        P("dp", "tile", None, None),
    )
    out_specs = (P("dp", None, "tile", None), P(("dp", "tile"), None))
    return jax.shard_map(
        per_device, mesh=mesh, in_specs=in_specs, out_specs=out_specs, check_vma=False
    )
```

```python
import math

import jax
import jax.numpy as jnp
import ml_dtypes
import numpy as np
from jax import lax
from jax.experimental import pallas as pl
from jax.experimental.pallas import tpu as pltpu
from jax.sharding import PartitionSpec as P

MESH = pl.DeviceIdType.MESH
BF = jnp.bfloat16
F32 = jnp.float32

DIRS = ((-1, 0), (1, 0), (0, -1), (0, 1), (-1, -1), (-1, 1), (1, -1), (1, 1))
MAIN = (32, 32, 16, 16, 0, 0, 0, 0)
SIZE = tuple(4 * m + 16 for m in MAIN)
START = tuple(sum(SIZE[:d]) for d in range(8))
MAIN_AT = (0, 32, 64, 80)

CHUNK = 416
HEAD_ROWS = 26


def weight(cell, fine, cells, first, last):
    at = fine - 2 * cell
    value = 0.75 if at in (0, 1) else 0.25 if at in (-1, 2) else 0.0
    if first and cell == 0 and fine == 0:
        value += 0.25
    if last and cell == cells - 1 and fine == 2 * cells - 1:
        value += 0.25
    return value


def halo_cells(d):
    dr, dc = DIRS[d]
    rows = {1: [-1, 0], -1: [8, 7], 0: list(range(8))}[dr]
    cols = {1: [-1, 0], -1: [16, 15], 0: list(range(16))}[dc]
    if dr and dc:
        return [], [(j, w) for j in rows for w in cols]
    main = [(j, w) for j in rows for w in cols]
    if dr:
        corner = [(j, w) for j in rows for w in (-1, 16)]
    else:
        corner = [(j, w) for j in (-1, 8) for w in cols]
    return main, corner


def tables():
    send = np.zeros((9, 128, 512), np.float32)
    take = np.zeros((9, 480, 640), np.float32)
    for place in range(9):
        top, bottom = place // 3 == 0, place // 3 == 2
        left, right = place % 3 == 0, place % 3 == 2
        row_w = np.array([[weight(j, r, 8, top, bottom) for r in range(16)] for j in range(-1, 9)])
        col_w = np.array([[weight(w, c, 16, left, right) for c in range(32)] for w in range(-1, 17)])

        def line(j, w):
            return np.outer(row_w[j + 1], col_w[w + 1]).reshape(512)

        for d, (dr, dc) in enumerate(DIRS):
            main, corner = halo_cells(d)
            for m, (j, w) in enumerate(main):
                send[place, MAIN_AT[d] + m] = line(j + 8 * dr, w + 16 * dc)
            for m, (j, w) in enumerate(corner):
                send[place, 96 + 4 * d + m] = line(j + 8 * dr, w + 16 * dc)

        def outside(j, w):
            return (j < 0 and top) or (j > 7 and bottom) or (w < 0 and left) or (w > 15 and right)

        for shift in range(3):
            for jr in range(10):
                for ww in range(16):
                    j, w = jr - 1, shift + ww - 1
                    if not outside(j, w):
                        take[place, shift * 160 + jr * 16 + ww, :512] = line(j, w)
            for d in range(8):
                main, corner = halo_cells(d)
                at = [(512 + MAIN_AT[d] + m, cell) for m, cell in enumerate(main)] if main else []
                at += [(608 + 4 * d + m, cell) for m, cell in enumerate(corner)]
                for column, (j, w) in at:
                    ww = w + 1 - shift
                    if 0 <= ww < 16 and not outside(j, w):
                        take[place, shift * 160 + (j + 1) * 16 + ww, column] = 1.0
    order = np.zeros((128, 128), np.float32)
    for i in range(4):
        for d in range(8):
            for cell in range(4):
                order[d * 16 + i * 4 + cell, i * 32 + d * 4 + cell] = 1.0
    as_bf16 = [a.astype(ml_dtypes.bfloat16) for a in (send, take, np.stack([order, order.T]))]
    return as_bf16


def mm(a, b):
    return jnp.dot(a, b, preferred_element_type=F32)


def mm_t(a, b):
    return lax.dot_general(a, b, (((1,), (1,)), ((), ())), preferred_element_type=F32)


def kernel(
    cot_hbm, saved_hbm, feat_hbm, w_hbm, proj_hbm, send_hbm, take_hbm, order_hbm,
    fg_out, head_out,
    cot, saved, feat, wconv, proj, send_m, take_m, order_m,
    saved_t, feat_t, halo_out, halo_in, corner, acc, pooled, grad_acc, grad, tok, fg,
    head, send_c, recv_c, part, split_1, send_1, recv_1, split_2, send_2, recv_2, kept, last, send_3, recv_3,
    load_sem, halo_ss, halo_rs, tok_ss, tok_rs, c_ss, c_rs, ss_1, rs_1, ss_2, rs_2, ss_3, rs_3, out_sem,
):
    dp = lax.axis_index("dp")
    tile = lax.axis_index("tile")
    z, y, xh, core = tile // 16, (tile // 4) % 4, (tile // 2) % 2, tile % 2
    x = xh * 2 + dp
    g, row = tile % 8, tile // 8
    g0, g1, g2 = g % 2, (g // 2) % 2, g // 4
    col = g2 * 4 + (g2 + g1) % 2 * 2 + (g2 + g1 + g0) % 2
    a = jnp.where(core == 0, x, y)
    b = jnp.where(core == 0, y, x)

    def gray(c):
        c0, c1, c2 = c % 2, (c // 2) % 2, c // 4
        return c2 * 4 + (c2 + c1) % 2 * 2 + (c1 + c0) % 2

    beside_x, beside_y = z * 16 + y * 4 + core, z * 16 + xh * 2 + core

    def in_plane(to_x, to_y, along_x):
        return {
            "dp": jnp.where(along_x, to_x % 2, dp),
            "tile": jnp.where(along_x, beside_x + to_x // 2 * 2, beside_y + to_y * 4),
        }

    def remote(src, dst, send_sem, recv_sem, device):
        return pltpu.make_async_remote_copy(
            src_ref=src, dst_ref=dst, send_sem=send_sem, recv_sem=recv_sem,
            device_id=device, device_id_type=MESH,
        )

    place = (
        jnp.where(row == 0, 0, jnp.where(row == 15, 2, 1)) * 3
        + jnp.where(col == 0, 0, jnp.where(col == 7, 2, 1))
    )
    loads = [
        pltpu.make_async_copy(src, dst, load_sem.at[n])
        for n, (src, dst) in enumerate([
            (cot_hbm, cot), (send_hbm.at[place], send_m), (order_hbm, order_m),
            (take_hbm.at[place], take_m), (saved_hbm, saved), (w_hbm, wconv), (feat_hbm, feat),
            (proj_hbm, proj),
        ])
    ]
    for load in loads[:4]:
        load.start()

    barrier = pltpu.get_barrier_semaphore()

    def greet(device):
        pl.semaphore_signal(barrier, inc=1, device_id=device, device_id_type=MESH)

    def has(dr, dc):
        to_row, to_col = row + dr, col + dc
        ok = jnp.logical_and(to_row >= 0, to_row < 16)
        return jnp.logical_and(ok, jnp.logical_and(to_col >= 0, to_col < 8))

    def beside(dr, dc):
        return jnp.clip(row + dr, 0, 15) * 8 + gray(jnp.clip(col + dc, 0, 7))

    greeted = jnp.int32(0)
    for dr, dc in DIRS:
        if dr:

            @pl.when(has(dr, dc))
            def _():
                greet({"tile": beside(dr, dc)})

            greeted = greeted + has(dr, dc).astype(jnp.int32)
    for n in range(1, 8):
        greet({"tile": row * 8 + (g + n) % 8})
    for n in range(2):
        greet({"dp": 1 - dp, "tile": z * 16 + y * 4 + n * 2 + core})
        greet({"tile": z * 16 + (y // 2 * 2 + 2 + n) % 4 * 4 + xh * 2 + core})
    for n in range(1, 8):
        for c in range(2):
            greet({"tile": (z + n) % 8 * 16 + y * 4 + xh * 2 + c})
    greeted = greeted + 25

    for n in range(3):
        loads[n].wait()
    for load in loads[4:]:
        load.start()
    for i in range(4):
        r = mm(send_m[...], cot[i]).astype(BF)
        for d in range(4):
            m = MAIN[d]
            halo_out[START[d] + i * m : START[d] + (i + 1) * m, :] = r[MAIN_AT[d] : MAIN_AT[d] + m]
        corner[i * 32 : (i + 1) * 32, :] = r[96:128]
    corners = mm(order_m[0], corner[...]).astype(BF)
    for d in range(8):
        halo_out[START[d] + 4 * MAIN[d] : START[d] + SIZE[d], :] = corners[d * 16 : d * 16 + 16]

    def halo(d):
        return remote(
            halo_out.at[START[d] : START[d] + SIZE[d]], halo_in.at[START[d] : START[d] + SIZE[d]],
            halo_ss.at[d], halo_rs.at[d], {"tile": beside(*DIRS[d])},
        )

    pl.semaphore_wait(barrier, greeted)
    for d in range(8):
        dr, dc = DIRS[d]

        @pl.when(has(dr, dc))
        def _():
            halo(d).start()

        @pl.when(jnp.logical_not(has(-dr, -dc)))
        def _():
            halo_in[START[d] : START[d] + SIZE[d], :] = jnp.zeros((SIZE[d], 256), BF)

    loads[3].wait()
    for i in range(4):
        acc[i] = mm(take_m[:, :512], cot[i])
    loads[4].wait()
    for k in range(2):
        for i in range(4):
            saved_t[k * 256 : (k + 1) * 256, i * 128 : (i + 1) * 128] = saved[i, k].T

    for d in range(8):
        dr, dc = DIRS[d]

        @pl.when(has(-dr, -dc))
        def _():
            halo(d).wait_recv()

    for d in range(8):
        at = START[d] + 4 * MAIN[d]
        corner[d * 16 : d * 16 + 16, :] = halo_in[at : at + 16, :]
    corners = mm(order_m[1], corner[...]).astype(BF)
    for i in range(4):
        parts = [halo_in[START[d] + i * MAIN[d] : START[d] + (i + 1) * MAIN[d], :] for d in range(4)]
        ring = jnp.concatenate(parts + [corners[i * 32 : (i + 1) * 32]], axis=0)
        full = (acc[i] + mm(take_m[:, 512:], ring)).astype(BF)
        for shift in range(3):
            pooled[shift, i] = full[shift * 160 : (shift + 1) * 160]

    def tap(t):
        u, v = t // 3, t % 3
        return pooled[2 - v, :, (2 - u) * 16 : (2 - u) * 16 + 128, :].reshape(512, 256)

    def regroup(k, n):
        there = (g + n) % 8
        return remote(
            grad.at[k, :, pl.ds(pl.multiple_of(there * 16, 16), 16)],
            tok.at[k, :, pl.ds(pl.multiple_of(col * 16, 16), 16)],
            tok_ss.at[k, n], tok_rs.at[k, n], {"tile": row * 8 + there},
        )

    loads[5].wait()
    for k in range(2):
        for t in range(9):
            term = mm_t(tap(t), wconv[k * 9 + t])
            if t == 0:
                grad_acc[...] = term
            elif t < 8:
                grad_acc[...] += term
            else:
                grad[k] = (grad_acc[...] + term).astype(BF).reshape(4, 128, 256)
        for n in range(1, 8):
            regroup(k, n).start()
        tok[k, :, pl.ds(pl.multiple_of(col * 16, 16), 16)] = grad[k, :, pl.ds(pl.multiple_of(g * 16, 16), 16)]

    mine = pl.ds(pl.multiple_of(core * 128, 128), 128)
    theirs = pl.ds(pl.multiple_of((1 - core) * 128, 128), 128)
    pair_device = {"tile": tile + 1 - 2 * core}

    def swap(q):
        return remote(send_c.at[q], recv_c.at[q], c_ss.at[q], c_rs.at[q], pair_device)

    def to_first(pair, n):
        return jnp.where(core == 0, pair // 4 + n % 2 * 2, n)

    def first(pair, n):
        to_a = to_first(pair, n)
        slot = jnp.where(core == 0, pair % 4 * 2 + n // 2, pair)
        step = lax.rem(to_a - a + 3, 4)
        return remote(
            send_1.at[pair, n], recv_1.at[slot, step], ss_1.at[pair, n], rs_1.at[slot, step],
            in_plane(pair // 4 + n % 2 * 2, n, core == 0),
        )

    def ready(q):
        send_c[q] = head[q * CHUNK : (q + 1) * CHUNK, theirs].astype(BF)
        swap(q).start()

    def reduced(pair):
        for q in (2 * pair, 2 * pair + 1):
            swap(q).wait_recv()
            part[q] = head[q * CHUNK : (q + 1) * CHUNK, mine] + recv_c[q].astype(F32)

        @pl.when(core == 0)
        def _():
            for n in range(4):
                for p in range(4):
                    at = p * 104 + n % 2 * 52
                    split_1[pair, n, p * 52 : p * 52 + 52, :] = part[2 * pair + n // 2, at : at + 52, :]

        @pl.when(core == 1)
        def _():
            for n in range(4):
                for h in range(2):
                    split_1[pair, n, h * 104 : h * 104 + 104, :] = part[2 * pair + h, n * 104 : n * 104 + 104, :]

        for n in range(4):
            send_1[pair, n] = split_1[pair, n].astype(BF)

            @pl.when(a != to_first(pair, n))
            def _():
                first(pair, n).start()

    def second(j, to_b):
        step = lax.rem(to_b - b + 3, 4)
        return remote(
            send_2.at[j, to_b], recv_2.at[j, step], ss_2.at[j, to_b], rs_2.at[j, step],
            in_plane(to_b, to_b, core == 1),
        )

    def to_second(j):
        for h in range(2):
            e = jnp.where(core == 0, 2 * j + h, j + 4 * h)
            pair = jnp.where(core == 0, a % 2 * 4 + j, e)
            n = jnp.where(core == 0, h * 2 + a // 2, a)
            total = split_1[pair, n]
            for s in range(3):
                remote(
                    send_1.at[0, 0], recv_1.at[e, s], ss_1.at[0, 0], rs_1.at[e, s], pair_device
                ).wait_recv()
                total = total + recv_1[e, s].astype(F32)
            kept[j, h] = total

        @pl.when(core == 0)
        def _():
            for to_b in range(4):
                for h in range(2):
                    split_2[j, to_b, h * 52 : h * 52 + 52, :] = kept[j, h, to_b * 52 : to_b * 52 + 52, :]

        @pl.when(core == 1)
        def _():
            for to_b in range(4):
                for h in range(2):
                    at = h * 104 + to_b // 2 * 52
                    split_2[j, to_b, h * 52 : h * 52 + 52, :] = kept[j, to_b % 2, at : at + 52, :]

        for to_b in range(4):
            split_2[j, to_b, 104:112, :] = jnp.zeros((8, 128), F32)
            send_2[j, to_b] = split_2[j, to_b].astype(BF)

            @pl.when(b != to_b)
            def _():
                second(j, to_b).start()

    def third(p):
        return remote(
            send_3.at[p], recv_3.at[z, core], ss_3.at[p], rs_3.at[z, core],
            {"tile": p // 2 * 16 + y * 4 + xh * 2 + p % 2},
        )

    def to_self(p):
        return jnp.logical_and(z == p // 2, core == p % 2)

    def to_third(j):
        total = split_2[j, b]
        for s in range(3):
            remote(
                send_2.at[0, 0], recv_2.at[j, s], ss_2.at[0, 0], rs_2.at[j, s], pair_device
            ).wait_recv()
            total = total + recv_2[j, s].astype(F32)
        last[j] = total
        for n in range(4):
            p = 4 * j + n
            send_3[p] = last[j, n * HEAD_ROWS : n * HEAD_ROWS + 32, :].astype(BF)

            @pl.when(jnp.logical_not(to_self(p)))
            def _():
                third(p).start()

            @pl.when(to_self(p))
            def _():
                recv_3[z, core] = send_3[p]

    for k in (1, 0):
        for t in range(9):
            at = 2048 + (k * 9 + t) * 256
            head[at : at + 256, :] = mm(saved_t[k * 256 : (k + 1) * 256, :], tap(t))
        for q in (range(5, 11), range(11, 16))[k]:
            ready(q)
    loads[6].wait()
    for k in range(2):
        for i in range(4):
            feat_t[k * 1024 : (k + 1) * 1024, i * 128 : (i + 1) * 128] = feat[i, k].T
    for pair in (7, 3, 4, 5, 6):
        reduced(pair)

    for k in range(2):
        for n in range(1, 8):
            regroup(k, n).wait_recv()
        for h in range(4):
            at = k * 1024 + h * 256
            head[at : at + 256, :] = mm(feat_t[at : at + 256, :], tok[k].reshape(512, 256))
        for q in (range(0, 2), range(2, 5))[k]:
            ready(q)
    reduced(0)
    to_second(3)
    reduced(1)
    reduced(2)

    loads[7].wait()
    for k in range(2):
        tokens = tok[k].reshape(512, 256)
        for n in range(4):
            fg[:, k, :, n * 256 : n * 256 + 256] = (
                mm_t(tokens, proj[k, n * 256 : n * 256 + 256]).astype(BF).reshape(4, 128, 256)
            )
    out_copy = pltpu.make_async_copy(fg, fg_out, out_sem)
    out_copy.start()

    to_second(0)
    to_third(3)
    to_second(1)
    to_third(0)
    to_second(2)
    to_third(1)
    to_third(2)

    for d in range(8):

        @pl.when(has(*DIRS[d]))
        def _():
            halo(d).wait_send()

    for k in range(2):
        for n in range(1, 8):
            regroup(k, n).wait_send()
    for q in range(16):
        swap(q).wait_send()
    for pair in range(8):
        for n in range(4):

            @pl.when(a != to_first(pair, n))
            def _():
                first(pair, n).wait_send()

    for j in range(4):
        for to_b in range(4):

            @pl.when(b != to_b)
            def _():
                second(j, to_b).wait_send()

    for p in range(16):

        @pl.when(jnp.logical_not(to_self(p)))
        def _():
            third(p).wait_send()

    out_copy.wait()

    for c in range(2):
        total = jnp.zeros((32, 128), F32)
        for zz in range(8):

            @pl.when(jnp.logical_not(to_self(zz * 2 + c)))
            def _():
                remote(
                    send_3.at[0], recv_3.at[zz, c], ss_3.at[0], rs_3.at[zz, c], pair_device
                ).wait_recv()

            total = total + recv_3[zz, c].astype(F32)
        head_out[:, c * 128 : (c + 1) * 128] = total[:HEAD_ROWS] * (1.0 / math.sqrt(8 * 16384))


def per_device(features, proj_weight, conv_weight, saved, cotangent):
    send, take, order = (jnp.asarray(t) for t in tables())
    hbm = pl.BlockSpec(memory_space=pltpu.HBM)
    whole = pl.BlockSpec(memory_space=pltpu.VMEM)
    dma = pltpu.SemaphoreType.DMA
    vmem = pltpu.VMEM
    return pl.pallas_call(
        kernel,
        out_shape=(
            jax.ShapeDtypeStruct((4, 2, 128, 1024), BF),
            jax.ShapeDtypeStruct((HEAD_ROWS, 256), F32),
        ),
        in_specs=[hbm] * 8,
        out_specs=(pl.BlockSpec(memory_space=pl.ANY), whole),
        scratch_shapes=[
            vmem((4, 512, 256), BF), vmem((4, 2, 128, 256), BF), vmem((4, 2, 128, 1024), BF),
            vmem((18, 256, 256), BF), vmem((2, 1024, 256), BF),
            vmem((128, 512), BF), vmem((480, 640), BF), vmem((2, 128, 128), BF),
            vmem((512, 512), BF), vmem((2048, 512), BF), vmem((512, 256), BF), vmem((512, 256), BF),
            vmem((128, 256), BF), vmem((4, 480, 256), F32), vmem((3, 4, 160, 256), BF),
            vmem((512, 256), F32), vmem((2, 4, 128, 256), BF), vmem((2, 4, 128, 256), BF),
            vmem((4, 2, 128, 1024), BF),
            vmem((6656, 256), F32), vmem((16, CHUNK, 128), BF), vmem((16, CHUNK, 128), BF),
            vmem((16, CHUNK, 128), F32), vmem((8, 4, 208, 128), F32), vmem((8, 4, 208, 128), BF),
            vmem((8, 3, 208, 128), BF), vmem((4, 4, 112, 128), F32), vmem((4, 4, 112, 128), BF),
            vmem((4, 3, 112, 128), BF), vmem((4, 2, 208, 128), F32), vmem((4, 112, 128), F32),
            vmem((16, 32, 128), BF), vmem((8, 2, 32, 128), BF),
            dma((8,)), dma((8,)), dma((8,)), dma((2, 8)), dma((2, 8)), dma((16,)), dma((16,)),
            dma((8, 4)), dma((8, 3)), dma((4, 4)), dma((4, 3)), dma((16,)), dma((8, 2)), dma,
        ],
        compiler_params=pltpu.CompilerParams(
            collective_id=0, has_side_effects=True, vmem_limit_bytes=56 * 2**20
        ),
        cost_estimate=pl.CostEstimate(flops=3_000_000_000, bytes_accessed=9_000_000, transcendentals=0),
        name="head_backward",
    )(
        cotangent.reshape(4, 512, 256),
        saved.reshape(4, 2, 128, 256),
        features,
        conv_weight.reshape(18, 256, 256),
        proj_weight,
        send,
        take,
        order,
    )


def solution(mesh):
    in_specs = (
        P("dp", None, "tile", None),
        P(),
        P(),
        P("dp", None, "tile", None, None),
        P("dp", "tile", None, None),
    )
    out_specs = (P("dp", None, "tile", None), P(("dp", "tile"), None))
    return jax.shard_map(
        per_device, mesh=mesh, in_specs=in_specs, out_specs=out_specs, check_vma=False
    )
```
